512 devices in a mesh: section: 32 (over z_lo, x, core), tensor: 16 (over z_hi, y).
Axes of the slice: x: 4, y: 8, z: 8 (z_hi: 2, z_lo: 4; z = z_hi * 4 + z_lo), core: 2. Of those that a mesh axis runs over, the one named last changes fastest.
Arguments:
- transit_latents: bfloat16 [32, 256, 512], P('section', None, 'tensor'), may hold values from -6 to 6
- encoded_arrivals: bfloat16 [2, 256, 512], P(None, None, 'tensor'), may hold values from -6 to 6
- arriving_latent_derivative: bfloat16 [32, 256, 512], P('section', None, 'tensor'), may hold values from -6 to 6
- objective_derivative_arrivals: bfloat16 [2, 256, 512], P(None, None, 'tensor'), may hold values from -6 to 6
- kept_inputs: bfloat16 [32, 3, 256, 512], P('section', None, None, 'tensor'), may hold values from -6 to 6
- onward_sequence_labels: int32 [34, 256], replicated, may hold values from 0 to 3, never falling along the last dimension, each value on 1 to 128 neighbouring positions
- reverse_sequence_labels: int32 [34, 256], replicated, may hold values from 0 to 3, never falling along the last dimension, each value on 1 to 128 neighbouring positions
- expander_attn_factors: bfloat16 [32, 512, 12288], P('section', None, 'tensor'), may hold values from -0.25 to 0.25
- outgoing_compressor_factors: bfloat16 [32, 4096, 512], P('section', 'tensor'), may hold values from -0.09375 to 0.09375
Outputs:
- codes_out: bfloat16 [32, 3, 256, 512], P('section', None, None, 'tensor')
- grads_out: bfloat16 [32, 3, 256, 512], P('section', None, None, 'tensor')
- grad_qkv: float32 [32, 512, 12288], P('section', None, 'tensor')
- grad_out: float32 [32, 4096, 512], P('section', 'tensor')
The draws below stay inside these ranges and needn't reach their ends.
Inputs may be any that keep to these rules, and one draw needn't show every extreme that they name: `onward_sequence_labels`: along each row the ids never fall; a document spans at most 128 tokens, and some document spans exactly that many. `reverse_sequence_labels`: along each row the ids never fall; a document spans at most 128 tokens, and some document spans exactly that many.
All inputs are finite; a program needn't handle non-finite values.
Results may differ from the reference program's by a relative error of at most 0.03.
Values may be sent and summed in bfloat16 or wider, within the bound.
A program may use at most 64 MiB of HBM per device.

```python
import math
import jax
import jax.numpy as jnp
import numpy as np
from jax import lax

LATENT_DIM = 512
HD = 128
SMALL_BATCH_LEN = 256
TICKS = 3
PASSING_PARTS = 32
HEADS = 32
NMB = 34


def block_scale(stream_key, dims, cuts, low, top_value):
    loudness, own = 1.0, jax.random.fold_in(stream_key, 6)
    for dim, shards_of in cuts:
        steps = jnp.exp(jax.random.uniform(jax.random.fold_in(own, dim), (shards_of,), jnp.float32, low / len(cuts), top_value / len(cuts)))
        loudness = loudness * jnp.repeat(steps, dims[dim] // shards_of).reshape([-1 if axis == dim else 1 for axis in range(len(dims))])
    return loudness


def split_up(number_of, total, reach, lean):
    portions = [(1 << 20) // math.isqrt(grade ** lean) + 1 for grade in range(2, number_of + 1)]
    spare, counts = total - reach - (number_of - 1), [1] * (number_of - 1)
    while spare > 0:
        movable = [i for i in range(number_of - 1) if counts[i] < reach]
        whole, remaining = sum([portions[i] for i in movable]), spare
        for i in movable:
            more = min(reach - counts[i], max(1, remaining * portions[i] // whole), spare)
            counts[i] = counts[i] + more
            spare = spare - more
    return np.array([reach] + counts)


def uneven_parts(key, number_of, total, most, slope):
    if number_of == 2:
        one = jax.random.randint(key, (), max(1, total - most), min(most, total - 1) + 1)
        return jnp.stack([one, total - one])
    lengths = jnp.asarray(split_up(number_of, total, most, slope), jnp.int32)
    pairs = (number_of - 1) // 2
    giver, receiver = lengths[1:1 + 2 * pairs:2], lengths[2:2 + 2 * pairs:2]
    slack = jnp.minimum(giver - 1, most - receiver)
    passed = jax.random.randint(jax.random.fold_in(key, 1), (pairs,), 0, 1 << 20) % (slack + 1)
    lengths = lengths.at[1:1 + 2 * pairs:2].set(giver - passed).at[2:2 + 2 * pairs:2].set(receiver + passed)
    return lengths[jax.random.permutation(jax.random.fold_in(key, 2), number_of)]


def scatter_about(own_key, extent, scale, limit, shards=(), held_as=jnp.bfloat16):
    values = scale * jax.random.normal(own_key, extent, jnp.float32)
    if shards:
        values = values * block_scale(own_key, extent, shards, -0.22, 0.18)
    return jnp.clip(values, -limit, limit).astype(held_as)


def setup_inputs(seed: int = 0) -> dict:
    streams_of = jax.random.split(jax.random.key(seed), 10)
    transit_latents = scatter_about(streams_of[0], (PASSING_PARTS, SMALL_BATCH_LEN, LATENT_DIM), 1.0, 6.0, ((0, 32), (2, 16)))
    encoded_arrivals = scatter_about(streams_of[1], (TICKS - 1, SMALL_BATCH_LEN, LATENT_DIM), 1.0, 6.0, ((2, 16),))
    arriving_latent_derivative = scatter_about(streams_of[2], (PASSING_PARTS, SMALL_BATCH_LEN, LATENT_DIM), 1.0, 6.0, ((0, 32), (2, 16)))
    objective_derivative_arrivals = scatter_about(streams_of[3], (TICKS - 1, SMALL_BATCH_LEN, LATENT_DIM), 1.0, 6.0, ((2, 16),))
    kept_inputs = scatter_about(streams_of[4], (PASSING_PARTS, TICKS, SMALL_BATCH_LEN, LATENT_DIM), 1.0, 6.0, ((0, 32), (3, 16)))
    onward_sequence_labels = jax.vmap(lambda own: jnp.searchsorted(jnp.cumsum(uneven_parts(own, 4, SMALL_BATCH_LEN, SMALL_BATCH_LEN // 2, 0)), jnp.arange(SMALL_BATCH_LEN), side="right"))(jax.random.split(streams_of[5], NMB)).reshape((NMB, SMALL_BATCH_LEN)).astype(jnp.int32)
    reverse_sequence_labels = jax.vmap(lambda own: jnp.searchsorted(jnp.cumsum(uneven_parts(own, 4, SMALL_BATCH_LEN, SMALL_BATCH_LEN // 2, 0)), jnp.arange(SMALL_BATCH_LEN), side="right"))(jax.random.split(streams_of[6], NMB)).reshape((NMB, SMALL_BATCH_LEN)).astype(jnp.int32)
    expander_attn_factors = scatter_about(streams_of[7], (PASSING_PARTS, LATENT_DIM, HEADS * 3 * HD), LATENT_DIM ** -0.5, 0.25, ((0, 32), (2, 16)))
    outgoing_compressor_factors = scatter_about(streams_of[8], (PASSING_PARTS, HEADS * HD, LATENT_DIM), (HEADS * HD) ** -0.5, 0.09375, ((0, 32), (1, 16)))
    return {"transit_latents": transit_latents, "encoded_arrivals": encoded_arrivals, "arriving_latent_derivative": arriving_latent_derivative, "objective_derivative_arrivals": objective_derivative_arrivals, "kept_inputs": kept_inputs, "onward_sequence_labels": onward_sequence_labels, "reverse_sequence_labels": reverse_sequence_labels, "expander_attn_factors": expander_attn_factors, "outgoing_compressor_factors": outgoing_compressor_factors}


attention_score_scale = 8.0
norm_eps = 1e-05
head_eps = 1e-06

def contract_heads(form, left, right):
    return jnp.einsum(form, left.astype(jnp.float32), right.astype(jnp.float32))

def norm_rows(value_rows, eps):
    factor = lax.rsqrt(lax.optimization_barrier(jnp.mean(value_rows * value_rows, axis=-1, keepdims=True)) + eps)
    return (value_rows * factor, factor)

def norm_back(grad, normed, factor):
    return factor * (grad - normed * lax.optimization_barrier(jnp.mean(grad * normed, axis=-1, keepdims=True)))

def attend(compact_interface_latents, expander_attn_factors, segs, head_entry_width):
    token_row_block = compact_interface_latents.shape[0]
    normed32, row_factor = norm_rows(compact_interface_latents.astype(jnp.float32), norm_eps)
    normed = normed32.astype(jnp.bfloat16)
    packed = jnp.dot(normed, expander_attn_factors, preferred_element_type=jnp.float32).astype(jnp.bfloat16)
    packed = packed.reshape(token_row_block, -1, 3, head_entry_width)
    query, keys, value_rows = (packed[:, :, 0], packed[:, :, 1], packed[:, :, 2])
    query32, query_factor = norm_rows(query.astype(jnp.float32), head_eps)
    keys32, keys_factor = norm_rows(keys.astype(jnp.float32), head_eps)
    normalized_query = query32.astype(jnp.bfloat16)
    normalized_keys = keys32.astype(jnp.bfloat16)
    score_matrix = contract_heads('ypz,vpz->pyv', normalized_query, normalized_keys) * (attention_score_scale / head_entry_width)
    position = jnp.arange(token_row_block, dtype=jnp.int32)
    allowed = (position[None, :] <= position[:, None]) & (segs[None, :] == segs[:, None])
    weights = jnp.where(allowed[None], jnp.exp(score_matrix), jnp.float32(0.0))
    probs = weights / lax.optimization_barrier(jnp.sum(weights, axis=-1, keepdims=True))
    backward_probabilities = probs.astype(jnp.bfloat16)
    mixed_value_rows = contract_heads('gra,agy->rgy', backward_probabilities, value_rows).astype(jnp.bfloat16).reshape(token_row_block, -1)
    return (normed32, row_factor, normed, query32, query_factor, normalized_query, keys32, keys_factor, normalized_keys, value_rows, probs, backward_probabilities, mixed_value_rows)

def forward_term(compact_interface_latents, expander_attn_factors, outgoing_compressor_factors, segs, head_entry_width):
    mixed_value_rows = attend(compact_interface_latents, expander_attn_factors, segs, head_entry_width)[-1]
    return jnp.dot(mixed_value_rows, outgoing_compressor_factors, preferred_element_type=jnp.float32)

def backward_terms(compact_interface_latents, grad, expander_attn_factors, outgoing_compressor_factors, segs, head_entry_width):
    normed32, row_factor, normed, query32, query_factor, normalized_query, keys32, keys_factor, normalized_keys, value_rows, probs, backward_probabilities, mixed_value_rows = attend(compact_interface_latents, expander_attn_factors, segs, head_entry_width)
    token_row_block = compact_interface_latents.shape[0]
    grad_wout = jnp.dot(mixed_value_rows.T, grad, preferred_element_type=jnp.float32)
    gradient_mixed_values = jnp.dot(grad, outgoing_compressor_factors.T, preferred_element_type=jnp.float32).astype(jnp.bfloat16)
    gradient_mixed_values = gradient_mixed_values.reshape(token_row_block, -1, head_entry_width)
    gradient_probabilities = contract_heads('ypz,vpz->pyv', gradient_mixed_values, value_rows)
    gradient_value_rows = contract_heads('qrp,rqf->pqf', backward_probabilities, gradient_mixed_values).astype(jnp.bfloat16)
    inner = lax.optimization_barrier(jnp.sum(probs * gradient_probabilities, axis=-1, keepdims=True))
    gradient_score_matrix = (probs * (gradient_probabilities - inner) * (attention_score_scale / head_entry_width)).astype(jnp.bfloat16)
    gradient_normed_query = contract_heads('gra,agy->rgy', gradient_score_matrix, normalized_keys)
    gradient_normed_keys = contract_heads('qrp,rqf->pqf', gradient_score_matrix, normalized_query)
    d_query = norm_back(gradient_normed_query, query32, query_factor).astype(jnp.bfloat16)
    d_keys = norm_back(gradient_normed_keys, keys32, keys_factor).astype(jnp.bfloat16)
    d_packed = jnp.stack([d_query, d_keys, gradient_value_rows], axis=2).reshape(token_row_block, -1)
    grad_wqkv = jnp.dot(normed.T, d_packed, preferred_element_type=jnp.float32)
    d_normed = jnp.dot(d_packed, expander_attn_factors.T, preferred_element_type=jnp.float32)
    return (norm_back(d_normed, normed32, row_factor), grad_wqkv, grad_wout)

def reference(transit_latents, encoded_arrivals, arriving_latent_derivative, objective_derivative_arrivals, kept_inputs, onward_sequence_labels, reverse_sequence_labels, expander_attn_factors, outgoing_compressor_factors):
    section_ids = jnp.arange(PASSING_PARTS, dtype=jnp.int32)
    compact_interface_latents = transit_latents
    grads_now = arriving_latent_derivative
    total_qkv = jnp.zeros(expander_attn_factors.shape, jnp.float32)
    total_out = jnp.zeros(outgoing_compressor_factors.shape, jnp.float32)
    codes_list = []
    grads_list = []
    for tick in range(TICKS):
        fseg = onward_sequence_labels[(tick - section_ids + PASSING_PARTS - 1).astype(jnp.int32)]
        bseg = reverse_sequence_labels[(tick + section_ids).astype(jnp.int32)]

        def forward_one(items):
            code, wq, wo, seg = items
            term = forward_term(code, wq, wo, seg, HD)
            return (code.astype(jnp.float32) + term).astype(jnp.bfloat16)

        def backward_one(items):
            saved, grad, wq, wo, seg = items
            d_term, gq, go = backward_terms(saved, grad, wq, wo, seg, HD)
            return ((grad.astype(jnp.float32) + d_term).astype(jnp.bfloat16), gq, go)
        produced = lax.map(forward_one, (compact_interface_latents, expander_attn_factors, outgoing_compressor_factors, fseg))
        returned, gq, go = lax.map(backward_one, (kept_inputs[:, tick], grads_now, expander_attn_factors, outgoing_compressor_factors, bseg))
        total_qkv = total_qkv + gq
        total_out = total_out + go
        codes_list.append(produced)
        grads_list.append(returned)
        if tick + 1 < TICKS:
            compact_interface_latents = jnp.concatenate([encoded_arrivals[tick][None], produced[:-1]], axis=0)
            grads_now = jnp.concatenate([returned[1:], objective_derivative_arrivals[tick][None]], axis=0)
    return (jnp.stack(codes_list, axis=1), jnp.stack(grads_list, axis=1), total_qkv, total_out)
```

```python
import functools

import jax
import jax.numpy as jnp
from jax import lax
from jax.experimental import pallas as pl
from jax.experimental.pallas import tpu as pltpu
from jax.sharding import PartitionSpec as P

HD = 128
SCALE = 8.0 / 128
NORM_EPS = 1e-05
HEAD_EPS = 1e-06
TICKS = 3
YS = 8
COPIES = 192
BF = jnp.bfloat16
F32 = jnp.float32


def mm(a, b):
    return jnp.dot(a, b, preferred_element_type=F32)


def mm_nt(a, b):
    return lax.dot_general(a, b, (((1,), (1,)), ((), ())), preferred_element_type=F32)


def kernel(
    sections,
    pieces_ref, flab_ref, blab_ref, w_ref, wo_ref,
    codes_ref, grads_ref, gq_ref, go_ref,
    full, part, rsb, zbuf, qsend, qown, qrecv,
    wt, wot, maskf, maskb,
    nt_s, q32_s, qn_s, kn_s, k32_s, v_s, p_s, pb_s, mix_s, fac_s, rr_s, dp_s,
    send_sems, recv_sems,
):
    feat, toks = 512, 256
    heads = w_ref.shape[1] // (3 * HD)
    s = lax.axis_index("section")
    rank = lax.axis_index("tensor")
    z = rank // YS
    y = rank % YS
    up, down = (y + 1) % YS, (y + YS - 1) % YS
    nxt, prv = (s + 1) % sections, (s + sections - 1) % sections

    def dev(sec, zz, yy):
        return {"section": sec, "tensor": zz * YS + yy}

    up_dev, down_dev, z_dev = dev(s, z, up), dev(s, z, down), dev(s, 1 - z, y)
    partners = (up_dev, down_dev, z_dev, dev(nxt, z, y), dev(nxt, 1 - z, y), dev(prv, z, y), dev(prv, 1 - z, y))
    barrier = pltpu.get_barrier_semaphore()
    for p in partners:
        pl.semaphore_signal(barrier, inc=1, device_id=p, device_id_type=pl.DeviceIdType.MESH)

    copies = []

    def send(src, dst, target):
        i = len(copies)
        c = pltpu.make_async_remote_copy(
            src_ref=src, dst_ref=dst, send_sem=send_sems.at[i], recv_sem=recv_sems.at[i],
            device_id=target, device_id_type=pl.DeviceIdType.MESH,
        )
        c.start()
        copies.append(c)
        return c

    def at(k):
        return (y + k + YS) % YS

    class Gather:
        def __init__(self, b):
            self.b = b

        def exchange(self, piece):
            full[self.b, z, y] = pieces_ref[piece]
            self.zc = send(full.at[self.b, z, y], full.at[self.b, z, y], z_dev)

        def start(self):
            ref = full.at[self.b, :, y]
            self.plus, self.minus = send(ref, ref, up_dev), send(ref, ref, down_dev)

        def step(self, k):
            self.plus.wait_recv()
            if k < 3:
                ref = full.at[self.b, :, at(-k)]
            else:
                ref = full.at[self.b, 0, at(-k)]
            self.plus = send(ref, ref, up_dev)
            self.minus.wait_recv()
            if k < 3:
                ref = full.at[self.b, :, at(k)]
            else:
                ref = full.at[self.b, 1, at(k)]
            self.minus = send(ref, ref, down_dev)

        def finish(self):
            self.plus.wait_recv()
            self.minus.wait_recv()

    class Reduce:
        def __init__(self, c, t):
            self.p = part.at[c, t]
            self.r = rsb.at[c, t]

        def start(self):
            self.plus = send(self.p.at[0, at(4)], self.r.at[0, 0, 0], up_dev)
            self.minus = send(self.p.at[1, at(-4)], self.r.at[1, 0, 1], down_dev)

        def step(self, k):
            p, r = self.p, self.r
            for d, copy, target, own in ((0, self.plus, up_dev, at(4 - k)), (1, self.minus, down_dev, at(k - 4))):
                copy.wait_recv()
                if k == 1:
                    r[d, 0, d] = r[d, 0, d] + p[d, own]
                    r[d, 0, 1 - d] = p[1 - d, own]
                else:
                    r[d, k - 1] = r[d, k - 1] + p[:, own]
                new = send(r.at[d, k - 1], r.at[d, k], target)
                if d == 0:
                    self.plus = new
                else:
                    self.minus = new

        def finish(self):
            self.plus.wait_recv()
            self.minus.wait_recv()
            return self.r[0, 3].astype(F32) + self.r[1, 3].astype(F32) + self.p[:, y].astype(F32)

    outs = []

    class Pass:
        def __init__(self, c, t):
            self.c, self.t = c, t

        def start(self, total, b):
            c, t = self.c, self.t
            zero = jnp.zeros((32, toks), F32)
            halves = []
            for h in range(2):
                halves.append((total[h] + jnp.where(z == h, full[b, h, y].astype(F32), zero)).astype(BF))
            qown[c, t, 0] = halves[0]
            qown[c, t, 1] = halves[1]
            outs.append((c, t, send(qown.at[c, t, 1 - z], qrecv.at[c, t], z_dev)))
            if t + 1 < TICKS:
                edge = (s == sections - 1) if c == 0 else (s == 0)
                entering = pieces_ref[(5 if c == 0 else 7) + t]
                none = jnp.zeros((32, toks), BF)
                for h in range(2):
                    own_half = jnp.where(z == h, entering, none)
                    qsend[c, t, h] = jnp.where(edge, own_half, halves[h])
                to = nxt if c == 0 else prv
                self.near = send(qsend.at[c, t], zbuf.at[c, t, 0], dev(to, z, y))
                self.far = send(qsend.at[c, t], zbuf.at[c, t, 1], dev(to, 1 - z, y))

        def arrive(self, b):
            self.near.wait_recv()
            self.far.wait_recv()
            c, t = self.c, self.t
            full[b, :, y] = (zbuf[c, t, 0].astype(F32) + zbuf[c, t, 1].astype(F32)).astype(BF)

    def slot(kind, t):
        return kind * TICKS + t

    def make_mask(ref, row, out, t):
        seg = jnp.broadcast_to(ref[pl.ds(row, 1), :].astype(F32), (toks, toks))
        segt = seg.T
        j = lax.broadcasted_iota(jnp.int32, (toks, toks), 0)
        i = lax.broadcasted_iota(jnp.int32, (toks, toks), 1)
        out[t] = jnp.where((j <= i) & (seg == segt), 1.0, 0.0)

    def normed(b):
        a = full[b].reshape(feat, toks).astype(F32)
        rr = lax.rsqrt(jnp.mean(a * a, axis=0, keepdims=True) + NORM_EPS)
        return a * rr, rr

    def head_norm(x):
        f = lax.rsqrt(jnp.mean(x * x, axis=0, keepdims=True) + HEAD_EPS)
        return x * f, f

    def probs(qn, kn, mask):
        w = jnp.exp(mm(kn, qn) * SCALE) * mask
        return w * (1.0 / jnp.sum(w, axis=0, keepdims=True))

    def forward(t):
        n32, _ = normed(slot(0, t))
        packed = mm(wt[...], n32.astype(BF)).astype(BF)
        mask = maskf[t]
        mixed = []
        for h in range(heads):
            base = 3 * HD * h
            q32, _ = head_norm(packed[base:base + HD].astype(F32))
            k32, _ = head_norm(packed[base + HD:base + 2 * HD].astype(F32))
            p = probs(q32.astype(BF), k32.astype(BF).T, mask)
            mixed.append(mm(packed[base + 2 * HD:base + 3 * HD], p.astype(BF)).astype(BF))
        term = mm(wot[...], jnp.concatenate(mixed, axis=0))
        part[0, t] = term.astype(BF).reshape(2, YS, 32, toks)

    def recompute(t):
        n32, rr = normed(slot(2, t))
        n = n32.astype(BF)
        nt_s[t] = n
        rr_s[t] = rr
        packed = mm(wt[...], n).astype(BF)
        mask = maskb[t]
        for h in range(heads):
            base = 3 * HD * h
            q32, sq = head_norm(packed[base:base + HD].astype(F32))
            k32, sk = head_norm(packed[base + HD:base + 2 * HD].astype(F32))
            v = packed[base + 2 * HD:base + 3 * HD]
            q32_s[t, h], k32_s[t, h] = q32, k32
            fac_s[t, h, 0:1], fac_s[t, h, 1:2] = sq, sk
            qn, kn = q32.astype(BF), k32.astype(BF)
            qn_s[t, h], kn_s[t, h] = qn, kn
            v_s[t, h] = v.T
            p = probs(qn, kn.T, mask)
            p_s[t, h] = p
            pb = p.astype(BF)
            pb_s[t, h] = pb
            mix_s[t, h * HD:(h + 1) * HD] = mm(v, pb).astype(BF)

    def norm_back(grad, unit, factor):
        return factor * (grad - unit * jnp.mean(grad * unit, axis=0, keepdims=True))

    def back_head(t, h):
        g = full[slot(1, t)].reshape(feat, toks)
        dm = mm(wo_ref[h * HD:(h + 1) * HD], g).astype(BF)
        dp = mm(v_s[t, h], dm)
        base = 3 * HD * h
        pb = pb_s[t, h]
        dp_s[t, base + 2 * HD:base + 3 * HD] = mm_nt(dm, pb).astype(BF)
        p = p_s[t, h]
        pd = p * dp
        inner = jnp.sum(pd, axis=0, keepdims=True)
        ds = ((pd - p * inner) * SCALE).astype(BF)
        dq = mm(kn_s[t, h], ds)
        dk = mm_nt(qn_s[t, h], ds)
        dp_s[t, base:base + HD] = norm_back(dq, q32_s[t, h], fac_s[t, h, 0:1]).astype(BF)
        dp_s[t, base + HD:base + 2 * HD] = norm_back(dk, k32_s[t, h], fac_s[t, h, 1:2]).astype(BF)

    def back_term(t):
        dn = mm(w_ref[...], dp_s[t])
        rr = rr_s[t]
        n32 = full[slot(2, t)].reshape(feat, toks).astype(F32) * rr
        part[1, t] = norm_back(dn, n32, rr).astype(BF).reshape(2, YS, 32, toks)

    def weight_terms(t):
        g = full[slot(1, t)].reshape(feat, toks)
        gq = mm_nt(nt_s[t], dp_s[t])
        go = mm_nt(mix_s[t], g)
        if t == 0:
            gq_ref[...] = gq
            go_ref[...] = go
        else:
            gq_ref[...] += gq
            go_ref[...] += go

    wt[...] = w_ref[...].T
    wot[...] = wo_ref[...].T
    pl.semaphore_wait(barrier, len(partners))

    ag_f = Gather(slot(0, 0))
    ag_g = Gather(slot(1, 0))
    ag_s = [Gather(slot(2, t)) for t in range(TICKS)]
    ag_f.exchange(0)
    ag_s[0].exchange(2)
    ag_g.exchange(1)
    ag_s[1].exchange(3)
    ag_s[2].exchange(4)
    for t in range(TICKS):
        make_mask(flab_ref, t - s + sections - 1, maskf, t)
        make_mask(blab_ref, t + s, maskb, t)
    ag_f.zc.wait_recv()
    ag_f.start()
    ag_s[0].zc.wait_recv()
    ag_s[0].start()
    ag_g.zc.wait_recv()
    ag_g.start()
    for k in (1, 2, 3):
        ag_f.step(k)
        ag_s[0].step(k)
        ag_g.step(k)
    ag_s[1].zc.wait_recv()
    ag_s[2].zc.wait_recv()
    ag_f.finish()

    for t in range(TICKS):
        more = t + 1 < TICKS
        forward(t)
        rs_f = Reduce(0, t)
        rs_f.start()
        if t == 0:
            ag_s[0].finish()
            ag_g.finish()
        else:
            pass_b.arrive(slot(1, t))
            ag_g = Gather(slot(1, t))
            ag_g.start()
        recompute(t)
        rs_f.step(1)
        if t > 0:
            ag_g.step(1)
            rs_f.step(2)
            ag_g.step(2)
            rs_f.step(3)
            ag_g.step(3)
            ag_g.finish()
        back_head(t, 0)
        if t == 0:
            rs_f.step(2)
        back_head(t, 1)
        if t == 0:
            rs_f.step(3)
        pass_f = Pass(0, t)
        if t > 0:
            pass_f.start(rs_f.finish(), slot(0, t))
        back_term(t)
        rs_b = Reduce(1, t)
        rs_b.start()
        if t == 0:
            pass_f.start(rs_f.finish(), slot(0, t))
        weight_terms(t)
        rs_b.step(1)
        if more:
            pass_f.arrive(slot(0, t + 1))
            ag_f = Gather(slot(0, t + 1))
            ag_f.start()
            ag_s[t + 1].start()
        rs_b.step(2)
        if more:
            ag_f.step(1)
            ag_s[t + 1].step(1)
        rs_b.step(3)
        if more:
            ag_f.step(2)
            ag_s[t + 1].step(2)
        pass_b = Pass(1, t)
        pass_b.start(rs_b.finish(), slot(1, t))
        if more:
            ag_f.step(3)
            ag_s[t + 1].step(3)
            ag_f.finish()
            ag_s[t + 1].finish()

    for c, t, copy in outs:
        copy.wait_recv()
        out = codes_ref if c == 0 else grads_ref
        out[t] = (qown[c, t, z].astype(F32) + qrecv[c, t].astype(F32)).astype(BF)
    for c in copies:
        c.wait_send()


def body(
    transit_latents,
    encoded_arrivals,
    arriving_latent_derivative,
    objective_derivative_arrivals,
    kept_inputs,
    onward_sequence_labels,
    reverse_sequence_labels,
    expander_attn_factors,
    outgoing_compressor_factors,
):
    sections = lax.axis_size("section")
    w, wo = expander_attn_factors[0], outgoing_compressor_factors[0]
    feat, cols = w.shape
    heads = cols // (3 * HD)
    toks = transit_latents.shape[1]
    pieces = jnp.concatenate(
        [transit_latents, arriving_latent_derivative, kept_inputs[0], encoded_arrivals, objective_derivative_arrivals],
        axis=0,
    ).swapaxes(1, 2)
    shard = pieces.shape[1]
    vm = pl.BlockSpec(memory_space=pltpu.VMEM)
    block = (2, YS, shard, toks)
    scratch = [
        pltpu.VMEM((3 * TICKS,) + block, BF),
        pltpu.VMEM((2, TICKS) + block, BF),
        pltpu.VMEM((2, TICKS, 2, 4, 2, shard, toks), BF),
        pltpu.VMEM((2, TICKS, 2, 2, shard, toks), BF),
        pltpu.VMEM((2, TICKS, 2, shard, toks), BF),
        pltpu.VMEM((2, TICKS, 2, shard, toks), BF),
        pltpu.VMEM((2, TICKS, shard, toks), BF),
        pltpu.VMEM((cols, feat), BF),
        pltpu.VMEM((feat, heads * HD), BF),
        pltpu.VMEM((TICKS, toks, toks), F32),
        pltpu.VMEM((TICKS, toks, toks), F32),
        pltpu.VMEM((TICKS, feat, toks), BF),
        pltpu.VMEM((TICKS, heads, HD, toks), F32),
        pltpu.VMEM((TICKS, heads, HD, toks), BF),
        pltpu.VMEM((TICKS, heads, HD, toks), BF),
        pltpu.VMEM((TICKS, heads, HD, toks), F32),
        pltpu.VMEM((TICKS, heads, toks, HD), BF),
        pltpu.VMEM((TICKS, heads, toks, toks), F32),
        pltpu.VMEM((TICKS, heads, toks, toks), BF),
        pltpu.VMEM((TICKS, heads * HD, toks), BF),
        pltpu.VMEM((TICKS, heads, 8, toks), F32),
        pltpu.VMEM((TICKS, 1, toks), F32),
        pltpu.VMEM((TICKS, cols, toks), BF),
        pltpu.SemaphoreType.DMA((COPIES,)),
        pltpu.SemaphoreType.DMA((COPIES,)),
    ]
    codes, grads, gq, go = pl.pallas_call(
        functools.partial(kernel, sections),
        out_shape=(
            jax.ShapeDtypeStruct((TICKS, shard, toks), BF),
            jax.ShapeDtypeStruct((TICKS, shard, toks), BF),
            jax.ShapeDtypeStruct(w.shape, F32),
            jax.ShapeDtypeStruct(wo.shape, F32),
        ),
        in_specs=[vm] * 5,
        out_specs=(vm, vm, vm, vm),
        scratch_shapes=scratch,
        compiler_params=pltpu.CompilerParams(
            collective_id=0, has_side_effects=True, vmem_limit_bytes=48 * 1024 * 1024
        ),
    )(pieces, onward_sequence_labels, reverse_sequence_labels, w, wo)
    return codes.swapaxes(1, 2)[None], grads.swapaxes(1, 2)[None], gq[None], go[None]


def solution(mesh):
    in_specs = (
        P("section", None, "tensor"),
        P(None, None, "tensor"),
        P("section", None, "tensor"),
        P(None, None, "tensor"),
        P("section", None, None, "tensor"),
        P(),
        P(),
        P("section", None, "tensor"),
        P("section", "tensor", None),
    )
    out_specs = (
        P("section", None, None, "tensor"),
        P("section", None, None, "tensor"),
        P("section", None, "tensor"),
        P("section", "tensor", None),
    )
    return jax.shard_map(body, mesh=mesh, in_specs=in_specs, out_specs=out_specs, check_vma=False)
```

```python
import functools

import jax
import jax.numpy as jnp
from jax import lax
from jax.experimental import pallas as pl
from jax.experimental.pallas import tpu as pltpu
from jax.sharding import PartitionSpec as P

HD = 128
SCALE = 8.0 / 128
NORM_EPS = 1e-05
HEAD_EPS = 1e-06
TICKS = 3
YS = 8
COPIES = 192
BF = jnp.bfloat16
F32 = jnp.float32


def mm(a, b):
    return jnp.dot(a, b, preferred_element_type=F32)


def mm_nt(a, b):
    return lax.dot_general(a, b, (((1,), (1,)), ((), ())), preferred_element_type=F32)


def kernel(
    sections,
    codes_hbm, feed_hbm, grad_hbm, loss_hbm, kept_hbm, flab_hbm, blab_hbm, w_hbm, wo_hbm,
    codes_ref, grads_ref, gq_ref, go_ref,
    enter, flab_ref, blab_ref, w_ref, wo_ref,
    full, part, rsb, zbuf, qsend, qown, qrecv,
    wt, wot, maskf, maskb,
    nt_s, q32_s, qn_s, kn_s, k32_s, v_s, p_s, pb_s, mix_s, fac_s, rr_s, dp_s,
    load_sems, send_sems, recv_sems,
):
    feat, toks = 512, 256
    heads = w_ref.shape[1] // (3 * HD)
    s = lax.axis_index("section")
    rank = lax.axis_index("tensor")
    z = rank // YS
    y = rank % YS

    def at(k):
        return (y + k + YS) % YS

    nxt, prv = (s + 1) % sections, (s + sections - 1) % sections

    def dev(sec, zz, yy):
        return {"section": sec, "tensor": zz * YS + yy}

    ring = {k: dev(s, z, at(k)) for k in (1, -1, 2, -2)}
    z_dev = dev(s, 1 - z, y)
    partners = (*ring.values(), z_dev, dev(nxt, z, y), dev(nxt, 1 - z, y), dev(prv, z, y), dev(prv, 1 - z, y))
    barrier = pltpu.get_barrier_semaphore()
    for p in partners:
        pl.semaphore_signal(barrier, inc=1, device_id=p, device_id_type=pl.DeviceIdType.MESH)

    loads = []
    for src, dst in (
        (kept_hbm.at[0], full.at[pl.ds(2 * TICKS, TICKS), z, y]),
        (grad_hbm, full.at[pl.ds(TICKS, 1), z, y]),
        (codes_hbm, full.at[pl.ds(0, 1), z, y]),
        (w_hbm.at[0], w_ref),
        (wo_hbm.at[0], wo_ref),
        (blab_hbm, blab_ref),
        (flab_hbm, flab_ref),
        (feed_hbm, enter.at[0]),
        (loss_hbm, enter.at[1]),
    ):
        load = pltpu.make_async_copy(src, dst, load_sems.at[len(loads)])
        load.start()
        loads.append(load)

    copies = []

    def send(src, dst, target):
        i = len(copies)
        c = pltpu.make_async_remote_copy(
            src_ref=src, dst_ref=dst, send_sem=send_sems.at[i], recv_sem=recv_sems.at[i],
            device_id=target, device_id_type=pl.DeviceIdType.MESH,
        )
        c.start()
        copies.append(c)
        return c

    class Gather:
        def __init__(self, b, half=None):
            if half is None:
                self.block = lambda k: full.at[b, :, at(k)]
                self.parts = lambda k, h: full.at[b, h, at(k)]
            else:
                self.block = lambda k: full.at[b, half, at(k)]
                self.parts = lambda k, h: full.at[b, half, at(k), pl.ds(16 * h, 16)]

        def start(self):
            own = self.block(0)
            self.two = [send(own, own, ring[2]), send(own, own, ring[-2])]
            self.rest = [send(own, own, ring[1]), send(own, own, ring[-1])]

        def mid(self):
            for i, d in enumerate((1, -1)):
                self.two[i].wait_recv()
                far = self.parts(-2 * d, i)
                self.rest.append(send(far, far, ring[2 * d]))
                block = self.block(-2 * d)
                self.rest.append(send(block, block, ring[d]))

        def finish(self):
            for c in self.rest:
                c.wait_recv()

    class Reduce:
        def __init__(self, c, t):
            self.p = part.at[c, t]
            self.r = rsb.at[c, t]

        def start(self):
            p, r = self.p, self.r
            self.first = []
            for i, d in enumerate((1, -1)):
                far = send(p.at[i, at(4 * d)], r.at[i, 1, i], ring[2 * d])
                self.first.append((far, send(p.at[:, at(3 * d)], r.at[i, 0], ring[d])))
            self.rest = [send(p.at[:, at(d)], r.at[i, 3], ring[d]) for i, d in enumerate((1, -1))]

        def mid(self):
            p, r = self.p, self.r
            for i, d in enumerate((1, -1)):
                for c in self.first[i]:
                    c.wait_recv()
                own = at(2 * d)
                both = r[i, 0, i].astype(F32) + r[i, 1, i].astype(F32) + p[i, own].astype(F32)
                r[i, 0, i] = both.astype(BF)
                r[i, 0, 1 - i] = r[i, 0, 1 - i] + p[1 - i, own]
                self.rest.append(send(r.at[i, 0], r.at[i, 2], ring[2 * d]))

        def finish(self):
            for c in self.rest:
                c.wait_recv()
            r = self.r
            total = self.p[:, y].astype(F32)
            for i in range(2):
                total = total + r[i, 2].astype(F32) + r[i, 3].astype(F32)
            return total

    outs = []

    class Pass:
        def __init__(self, c, t):
            self.c, self.t = c, t

        def start(self, total, b):
            c, t = self.c, self.t
            zero = jnp.zeros((32, toks), F32)
            halves = []
            for h in range(2):
                halves.append((total[h] + jnp.where(z == h, full[b, h, y].astype(F32), zero)).astype(BF))
            qown[c, t, 0] = halves[0]
            qown[c, t, 1] = halves[1]
            if t + 1 < TICKS:
                edge = (s == sections - 1) if c == 0 else (s == 0)
                entering = enter[c, t]
                none = jnp.zeros((32, toks), BF)
                for h in range(2):
                    own_half = jnp.where(z == h, entering, none)
                    qsend[c, t, h] = jnp.where(edge, own_half, halves[h])
                to = nxt if c == 0 else prv
                self.far = send(qsend.at[c, t], zbuf.at[c, t, 1], dev(to, 1 - z, y))
                self.near = send(qsend.at[c, t], zbuf.at[c, t, 0], dev(to, z, y))
            outs.append((c, t, send(qown.at[c, t, 1 - z], qrecv.at[c, t], z_dev)))

        def arrive(self, b):
            self.near.wait_recv()
            self.far.wait_recv()
            c, t = self.c, self.t
            full[b, :, y] = (zbuf[c, t, 0].astype(F32) + zbuf[c, t, 1].astype(F32)).astype(BF)

    def slot(kind, t):
        return kind * TICKS + t

    def make_mask(ref, row, out, t):
        seg = jnp.broadcast_to(ref[pl.ds(row, 1), :].astype(F32), (toks, toks))
        segt = seg.T
        j = lax.broadcasted_iota(jnp.int32, (toks, toks), 0)
        i = lax.broadcasted_iota(jnp.int32, (toks, toks), 1)
        out[t] = jnp.where((j <= i) & (seg == segt), 1.0, 0.0)

    def normed(b):
        a = full[b].reshape(feat, toks).astype(F32)
        rr = lax.rsqrt(jnp.mean(a * a, axis=0, keepdims=True) + NORM_EPS)
        return a * rr, rr

    def head_norm(x):
        f = lax.rsqrt(jnp.mean(x * x, axis=0, keepdims=True) + HEAD_EPS)
        return x * f, f

    def probs(qn, kn, mask):
        w = jnp.exp(mm(kn, qn) * SCALE) * mask
        return w * (1.0 / jnp.sum(w, axis=0, keepdims=True))

    def forward(t):
        n32, _ = normed(slot(0, t))
        packed = mm(wt[...], n32.astype(BF)).astype(BF)
        mask = maskf[t]
        mixed = []
        for h in range(heads):
            base = 3 * HD * h
            q32, _ = head_norm(packed[base:base + HD].astype(F32))
            k32, _ = head_norm(packed[base + HD:base + 2 * HD].astype(F32))
            p = probs(q32.astype(BF), k32.astype(BF).T, mask)
            mixed.append(mm(packed[base + 2 * HD:base + 3 * HD], p.astype(BF)).astype(BF))
        term = mm(wot[...], jnp.concatenate(mixed, axis=0))
        part[0, t] = term.astype(BF).reshape(2, YS, 32, toks)

    def recompute(t):
        n32, rr = normed(slot(2, t))
        n = n32.astype(BF)
        nt_s[t] = n
        rr_s[t] = rr
        packed = mm(wt[...], n).astype(BF)
        mask = maskb[t]
        for h in range(heads):
            base = 3 * HD * h
            q32, sq = head_norm(packed[base:base + HD].astype(F32))
            k32, sk = head_norm(packed[base + HD:base + 2 * HD].astype(F32))
            v = packed[base + 2 * HD:base + 3 * HD]
            q32_s[t, h], k32_s[t, h] = q32, k32
            fac_s[t, h, 0:1], fac_s[t, h, 1:2] = sq, sk
            qn, kn = q32.astype(BF), k32.astype(BF)
            qn_s[t, h], kn_s[t, h] = qn, kn
            v_s[t, h] = v.T
            p = probs(qn, kn.T, mask)
            p_s[t, h] = p
            pb = p.astype(BF)
            pb_s[t, h] = pb
            mix_s[t, h * HD:(h + 1) * HD] = mm(v, pb).astype(BF)

    def norm_back(grad, unit, factor):
        return factor * (grad - unit * jnp.mean(grad * unit, axis=0, keepdims=True))

    def back_head(t, h):
        g = full[slot(1, t)].reshape(feat, toks)
        dm = mm(wo_ref[h * HD:(h + 1) * HD], g).astype(BF)
        dp = mm(v_s[t, h], dm)
        base = 3 * HD * h
        pb = pb_s[t, h]
        dp_s[t, base + 2 * HD:base + 3 * HD] = mm_nt(dm, pb).astype(BF)
        p = p_s[t, h]
        pd = p * dp
        inner = jnp.sum(pd, axis=0, keepdims=True)
        ds = ((pd - p * inner) * SCALE).astype(BF)
        dq = mm(kn_s[t, h], ds)
        dk = mm_nt(qn_s[t, h], ds)
        dp_s[t, base:base + HD] = norm_back(dq, q32_s[t, h], fac_s[t, h, 0:1]).astype(BF)
        dp_s[t, base + HD:base + 2 * HD] = norm_back(dk, k32_s[t, h], fac_s[t, h, 1:2]).astype(BF)

    def back_term(t):
        dn = mm(w_ref[...], dp_s[t])
        rr = rr_s[t]
        n32 = full[slot(2, t)].reshape(feat, toks).astype(F32) * rr
        part[1, t] = norm_back(dn, n32, rr).astype(BF).reshape(2, YS, 32, toks)

    def weight_terms(t):
        g = full[slot(1, t)].reshape(feat, toks)
        gq = mm_nt(nt_s[t], dp_s[t])
        go = mm_nt(mix_s[t], g)
        if t == 0:
            gq_ref[...] = gq
            go_ref[...] = go
        else:
            gq_ref[...] += gq
            go_ref[...] += go

    def backward(t):
        for h in range(heads):
            back_head(t, h)
        back_term(t)

    for load in loads[:3]:
        load.wait()
    pl.semaphore_wait(barrier, len(partners))

    order = [slot(2, 0), slot(1, 0), slot(0, 0)]
    across = {}
    for b in order + [slot(2, 1), slot(2, 2)]:
        across[b] = send(full.at[b, z, y], full.at[b, z, y], z_dev)
    mine = [Gather(b, z) for b in order]
    others = [Gather(b, 1 - z) for b in order]
    for g in mine:
        g.start()
    for load in loads[3:]:
        load.wait()
    wt[...] = w_ref[...].T
    wot[...] = wo_ref[...].T
    for g in mine:
        g.mid()
    make_mask(blab_ref, s, maskb, 0)
    make_mask(flab_ref, sections - 1 - s, maskf, 0)
    for b, g in zip(order, others):
        across[b].wait_recv()
        g.start()
    for t in range(1, TICKS):
        make_mask(blab_ref, t + s, maskb, t)
        make_mask(flab_ref, t - s + sections - 1, maskf, t)
    for g in mine:
        g.finish()
    for g in others:
        g.mid()
    others[0].finish()
    recompute(0)
    others[1].finish()

    reduce_b, reduce_f, pass_b, pass_f, kept = {}, {}, {}, {}, {}
    for t in range(TICKS):
        last = t + 1 == TICKS
        if t > 0:
            gather_b.finish()
            recompute(t)
        backward(t)
        reduce_b[t] = Reduce(1, t)
        reduce_b[t].start()
        if t == 0:
            others[2].finish()
        else:
            gather_f.mid()
        weight_terms(t)
        reduce_b[t].mid()
        if t > 0:
            gather_f.finish()
        forward(t)
        reduce_f[t] = Reduce(0, t)
        reduce_f[t].start()
        pass_b[t] = Pass(1, t)
        pass_b[t].start(reduce_b[t].finish(), slot(1, t))
        if not last:
            across[slot(2, t + 1)].wait_recv()
            kept = Gather(slot(2, t + 1))
            kept.start()
        reduce_f[t].mid()
        if not last:
            pass_b[t].arrive(slot(1, t + 1))
            gather_b = Gather(slot(1, t + 1))
            gather_b.start()
            kept.mid()
        pass_f[t] = Pass(0, t)
        pass_f[t].start(reduce_f[t].finish(), slot(0, t))
        if not last:
            gather_b.mid()
            pass_f[t].arrive(slot(0, t + 1))
            gather_f = Gather(slot(0, t + 1))
            gather_f.start()
            kept.finish()

    for c, t, copy in outs:
        copy.wait_recv()
        out = codes_ref if c == 0 else grads_ref
        out[t] = (qown[c, t, z].astype(F32) + qrecv[c, t].astype(F32)).astype(BF)
    for c in copies:
        c.wait_send()


def body(
    transit_latents,
    encoded_arrivals,
    arriving_latent_derivative,
    objective_derivative_arrivals,
    kept_inputs,
    onward_sequence_labels,
    reverse_sequence_labels,
    expander_attn_factors,
    outgoing_compressor_factors,
):
    sections = lax.axis_size("section")
    w, wo = jax.ShapeDtypeStruct(expander_attn_factors.shape[1:], BF), jax.ShapeDtypeStruct(outgoing_compressor_factors.shape[1:], BF)
    feat, cols = w.shape
    heads = cols // (3 * HD)
    toks, shard = transit_latents.shape[1:]
    vm = pl.BlockSpec(memory_space=pltpu.VMEM)
    block = (2, YS, shard, toks)
    hbm = pl.BlockSpec(memory_space=pl.ANY)
    scratch = [
        pltpu.VMEM((2, TICKS - 1, shard, toks), BF),
        pltpu.VMEM(onward_sequence_labels.shape, jnp.int32),
        pltpu.VMEM(reverse_sequence_labels.shape, jnp.int32),
        pltpu.VMEM((feat, cols), BF),
        pltpu.VMEM((heads * HD, feat), BF),
        pltpu.VMEM((3 * TICKS,) + block, BF),
        pltpu.VMEM((2, TICKS) + block, BF),
        pltpu.VMEM((2, TICKS, 2, 4, 2, shard, toks), BF),
        pltpu.VMEM((2, TICKS, 2, 2, shard, toks), BF),
        pltpu.VMEM((2, TICKS, 2, shard, toks), BF),
        pltpu.VMEM((2, TICKS, 2, shard, toks), BF),
        pltpu.VMEM((2, TICKS, shard, toks), BF),
        pltpu.VMEM((cols, feat), BF),
        pltpu.VMEM((feat, heads * HD), BF),
        pltpu.VMEM((TICKS, toks, toks), F32),
        pltpu.VMEM((TICKS, toks, toks), F32),
        pltpu.VMEM((TICKS, feat, toks), BF),
        pltpu.VMEM((TICKS, heads, HD, toks), F32),
        pltpu.VMEM((TICKS, heads, HD, toks), BF),
        pltpu.VMEM((TICKS, heads, HD, toks), BF),
        pltpu.VMEM((TICKS, heads, HD, toks), F32),
        pltpu.VMEM((TICKS, heads, toks, HD), BF),
        pltpu.VMEM((TICKS, heads, toks, toks), F32),
        pltpu.VMEM((TICKS, heads, toks, toks), BF),
        pltpu.VMEM((TICKS, heads * HD, toks), BF),
        pltpu.VMEM((TICKS, heads, 8, toks), F32),
        pltpu.VMEM((TICKS, 1, toks), F32),
        pltpu.VMEM((TICKS, cols, toks), BF),
        pltpu.SemaphoreType.DMA((9,)),
        pltpu.SemaphoreType.DMA((COPIES,)),
        pltpu.SemaphoreType.DMA((COPIES,)),
    ]
    codes, grads, gq, go = pl.pallas_call(
        functools.partial(kernel, sections),
        out_shape=(
            jax.ShapeDtypeStruct((TICKS, shard, toks), BF),
            jax.ShapeDtypeStruct((TICKS, shard, toks), BF),
            jax.ShapeDtypeStruct(w.shape, F32),
            jax.ShapeDtypeStruct(wo.shape, F32),
        ),
        in_specs=[hbm] * 9,
        out_specs=(vm, vm, vm, vm),
        scratch_shapes=scratch,
        compiler_params=pltpu.CompilerParams(
            collective_id=0, has_side_effects=True, vmem_limit_bytes=60 * 1024 * 1024
        ),
    )(
        transit_latents.swapaxes(1, 2),
        encoded_arrivals.swapaxes(1, 2),
        arriving_latent_derivative.swapaxes(1, 2),
        objective_derivative_arrivals.swapaxes(1, 2),
        kept_inputs.swapaxes(2, 3),
        onward_sequence_labels,
        reverse_sequence_labels,
        expander_attn_factors,
        outgoing_compressor_factors,
    )
    return codes.swapaxes(1, 2)[None], grads.swapaxes(1, 2)[None], gq[None], go[None]


def solution(mesh):
    in_specs = (
        P("section", None, "tensor"),
        P(None, None, "tensor"),
        P("section", None, "tensor"),
        P(None, None, "tensor"),
        P("section", None, None, "tensor"),
        P(),
        P(),
        P("section", None, "tensor"),
        P("section", "tensor", None),
    )
    out_specs = (
        P("section", None, None, "tensor"),
        P("section", None, None, "tensor"),
        P("section", None, "tensor"),
        P("section", "tensor", None),
    )
    return jax.shard_map(body, mesh=mesh, in_specs=in_specs, out_specs=out_specs, check_vma=False)
```

```python
import functools

import jax
import jax.numpy as jnp
from jax import lax
from jax.experimental import pallas as pl
from jax.experimental.pallas import tpu as pltpu
from jax.sharding import PartitionSpec as P

HD = 128
SCALE = 8.0 / 128
NORM_EPS = 1e-05
HEAD_EPS = 1e-06
TICKS = 3
YS = 8
COPIES = 352
BF = jnp.bfloat16
F32 = jnp.float32


def mm(a, b):
    return jnp.dot(a, b, preferred_element_type=F32)


def mm_nt(a, b):
    return lax.dot_general(a, b, (((1,), (1,)), ((), ())), preferred_element_type=F32)


def kernel(
    sections,
    codes_hbm, feed_hbm, grad_hbm, loss_hbm, kept_hbm, flab_hbm, blab_hbm, w_hbm, wo_hbm,
    out_ref, gq_ref, go_ref,
    enter, flab_ref, blab_ref, w_ref, wo_ref,
    full, part, rsb, zbuf, qsend, qown, qrecv,
    wt, wot, maskf, maskb,
    nt_s, q32_s, qn_s, kn_s, k32_s, v_s, p_s, pb_s, mix_s, fac_s, rr_s, dp_s,
    load_sems, send_sems, recv_sems,
):
    feat, toks = 512, 256
    heads = w_ref.shape[1] // (3 * HD)
    s = lax.axis_index("section")
    rank = lax.axis_index("tensor")
    z = rank // YS
    y = rank % YS

    def at(k):
        return (y + k + YS) % YS

    nxt, prv = (s + 1) % sections, (s + sections - 1) % sections

    def dev(sec, zz, yy):
        return {"section": sec, "tensor": zz * YS + yy}

    ring = {k: dev(s, z, at(k)) for k in (1, -1, 2, -2)}
    z_dev = dev(s, 1 - z, y)
    partners = (*ring.values(), z_dev, dev(nxt, z, y), dev(nxt, 1 - z, y), dev(prv, z, y), dev(prv, 1 - z, y))
    barrier = pltpu.get_barrier_semaphore()
    for p in partners:
        pl.semaphore_signal(barrier, inc=1, device_id=p, device_id_type=pl.DeviceIdType.MESH)

    loads = []
    for src, dst in (
        (kept_hbm.at[0], full.at[pl.ds(2 * TICKS, TICKS), z, y]),
        (grad_hbm, full.at[pl.ds(TICKS, 1), z, y]),
        (codes_hbm, full.at[pl.ds(0, 1), z, y]),
        (w_hbm.at[0], w_ref),
        (wo_hbm.at[0], wo_ref),
        (blab_hbm, blab_ref),
        (flab_hbm, flab_ref),
        (feed_hbm, enter.at[0]),
        (loss_hbm, enter.at[1]),
    ):
        load = pltpu.make_async_copy(src, dst, load_sems.at[len(loads)])
        load.start()
        loads.append(load)

    copies = []

    def send(src, dst, target):
        i = len(copies)
        c = pltpu.make_async_remote_copy(
            src_ref=src, dst_ref=dst, send_sem=send_sems.at[i], recv_sem=recv_sems.at[i],
            device_id=target, device_id_type=pl.DeviceIdType.MESH,
        )
        c.start()
        copies.append(c)
        return c

    class Gather:
        def __init__(self, b, h):
            self.block = lambda k: full.at[b, h, at(k)]
            self.parts = lambda k, i: full.at[b, h, at(k), pl.ds(16 * i, 16)]

        def start(self):
            own = self.block(0)
            self.two = [send(own, own, ring[2]), send(own, own, ring[-2])]
            self.rest = [send(own, own, ring[1]), send(own, own, ring[-1])]

        def mid(self):
            for i, d in enumerate((1, -1)):
                self.two[i].wait_recv()
                far = self.parts(-2 * d, i)
                self.rest.append(send(far, far, ring[2 * d]))
                block = self.block(-2 * d)
                self.rest.append(send(block, block, ring[d]))

        def finish(self):
            for c in self.rest:
                c.wait_recv()

    class Reduce:
        def __init__(self, c, t, h):
            self.h = h
            self.p = part.at[c, t, h]
            self.r = rsb.at[c, t, h]

        def start(self):
            p, r = self.p, self.r
            self.first = []
            for i, d in enumerate((1, -1)):
                rows = pl.ds(16 * i, 16)
                far = send(p.at[at(4 * d), rows], r.at[i, 1, rows], ring[2 * d])
                self.first.append((far, send(p.at[at(3 * d)], r.at[i, 0], ring[d])))
            self.rest = [send(p.at[at(d)], r.at[i, 3], ring[d]) for i, d in enumerate((1, -1))]

        def mid(self):
            p, r = self.p, self.r
            for i, d in enumerate((1, -1)):
                for c in self.first[i]:
                    c.wait_recv()
                both = r[i, 0].astype(F32) + p[at(2 * d)].astype(F32)
                far = r[i, 1, 16 * i:16 * i + 16].astype(F32)
                none = jnp.zeros_like(far)
                both = both + jnp.concatenate([far, none] if i == 0 else [none, far], axis=0)
                r[i, 0] = both.astype(BF)
                self.rest.append(send(r.at[i, 0], r.at[i, 2], ring[2 * d]))

        def finish(self):
            for c in self.rest:
                c.wait_recv()
            r = self.r
            total = self.p[y].astype(F32)
            for i in range(2):
                total = total + r[i, 2].astype(F32) + r[i, 3].astype(F32)
            return total

    outs = []

    class Pass:
        def __init__(self, c, t, h):
            self.c, self.t, self.h = c, t, h

        def start(self, total, b):
            c, t, h = self.c, self.t, self.h
            none = jnp.zeros((32, toks), F32)
            rows = (total + jnp.where(z == h, full[b, h, y].astype(F32), none)).astype(BF)
            qown[c, t, h] = rows
            if t + 1 < TICKS:
                edge = (s == sections - 1) if c == 0 else (s == 0)
                entering = jnp.where(z == h, enter[c, t], none.astype(BF))
                qsend[c, t, h] = jnp.where(edge, entering, rows)
                to = nxt if c == 0 else prv
                self.far = send(qsend.at[c, t, h], zbuf.at[c, t, 1, h], dev(to, 1 - z, y))
                self.near = send(qsend.at[c, t, h], zbuf.at[c, t, 0, h], dev(to, z, y))

        def arrive(self, b):
            self.near.wait_recv()
            self.far.wait_recv()
            c, t, h = self.c, self.t, self.h
            full[b, h, y] = (zbuf[c, t, 0, h].astype(F32) + zbuf[c, t, 1, h].astype(F32)).astype(BF)

    class Chain:
        def __init__(self, c, t):
            self.c, self.t = c, t
            self.halves = (0, 1) if t + 1 < TICKS else (1 - z, z)
            self.reduces = [Reduce(c, t, h) for h in self.halves]
            self.passes = [Pass(c, t, h) for h in self.halves]
            self.gathers = [Gather(slot(c, t + 1), h) for h in self.halves]

        def reduce_start(self):
            for r in self.reduces:
                r.start()

        def reduce_mid(self):
            for r in self.reduces:
                r.mid()

        def hand_over(self):
            c, t = self.c, self.t
            for i in range(2):
                self.passes[i].start(self.reduces[i].finish(), slot(c, t))
                if i == (0 if t + 1 == TICKS else 1):
                    outs.append((c, t, send(qown.at[c, t, 1 - z], qrecv.at[c, t], z_dev)))

        def gather_start(self):
            for i in range(2):
                self.passes[i].arrive(slot(self.c, self.t + 1))
                self.gathers[i].start()

        def gather_mid(self):
            for g in self.gathers:
                g.mid()

        def gather_finish(self):
            for g in self.gathers:
                g.finish()

    def slot(kind, t):
        return kind * TICKS + t

    def make_mask(ref, row, out, t):
        seg = jnp.broadcast_to(ref[pl.ds(row, 1), :].astype(F32), (toks, toks))
        segt = seg.T
        j = lax.broadcasted_iota(jnp.int32, (toks, toks), 0)
        i = lax.broadcasted_iota(jnp.int32, (toks, toks), 1)
        out[t] = jnp.where((j <= i) & (seg == segt), 1.0, 0.0)

    def normed(b):
        a = full[b].reshape(feat, toks).astype(F32)
        rr = lax.rsqrt(jnp.mean(a * a, axis=0, keepdims=True) + NORM_EPS)
        return a * rr, rr

    def head_norm(x):
        f = lax.rsqrt(jnp.mean(x * x, axis=0, keepdims=True) + HEAD_EPS)
        return x * f, f

    def probs(qn, kn, mask):
        w = jnp.exp(mm(kn, qn) * SCALE) * mask
        return w * (1.0 / jnp.sum(w, axis=0, keepdims=True))

    def forward(t):
        n32, _ = normed(slot(0, t))
        packed = mm(wt[...], n32.astype(BF)).astype(BF)
        mask = maskf[t]
        mixed = []
        for h in range(heads):
            base = 3 * HD * h
            q32, _ = head_norm(packed[base:base + HD].astype(F32))
            k32, _ = head_norm(packed[base + HD:base + 2 * HD].astype(F32))
            p = probs(q32.astype(BF), k32.astype(BF).T, mask)
            mixed.append(mm(packed[base + 2 * HD:base + 3 * HD], p.astype(BF)).astype(BF))
        term = mm(wot[...], jnp.concatenate(mixed, axis=0))
        part[0, t] = term.astype(BF).reshape(2, YS, 32, toks)

    def recompute(t):
        n32, rr = normed(slot(2, t))
        n = n32.astype(BF)
        nt_s[t] = n
        rr_s[t] = rr
        packed = mm(wt[...], n).astype(BF)
        mask = maskb[t]
        for h in range(heads):
            base = 3 * HD * h
            q32, sq = head_norm(packed[base:base + HD].astype(F32))
            k32, sk = head_norm(packed[base + HD:base + 2 * HD].astype(F32))
            v = packed[base + 2 * HD:base + 3 * HD]
            q32_s[t, h], k32_s[t, h] = q32, k32
            fac_s[t, h, 0:1], fac_s[t, h, 1:2] = sq, sk
            qn, kn = q32.astype(BF), k32.astype(BF)
            qn_s[t, h], kn_s[t, h] = qn, kn
            v_s[t, h] = v.T
            p = probs(qn, kn.T, mask)
            p_s[t, h] = p
            pb = p.astype(BF)
            pb_s[t, h] = pb
            mix_s[t, h * HD:(h + 1) * HD] = mm(v, pb).astype(BF)

    def norm_back(grad, unit, factor):
        return factor * (grad - unit * jnp.mean(grad * unit, axis=0, keepdims=True))

    def back_head(t, h):
        g = full[slot(1, t)].reshape(feat, toks)
        dm = mm(wo_ref[h * HD:(h + 1) * HD], g).astype(BF)
        dp = mm(v_s[t, h], dm)
        base = 3 * HD * h
        pb = pb_s[t, h]
        dp_s[t, base + 2 * HD:base + 3 * HD] = mm_nt(dm, pb).astype(BF)
        p = p_s[t, h]
        pd = p * dp
        inner = jnp.sum(pd, axis=0, keepdims=True)
        ds = ((pd - p * inner) * SCALE).astype(BF)
        dq = mm(kn_s[t, h], ds)
        dk = mm_nt(qn_s[t, h], ds)
        dp_s[t, base:base + HD] = norm_back(dq, q32_s[t, h], fac_s[t, h, 0:1]).astype(BF)
        dp_s[t, base + HD:base + 2 * HD] = norm_back(dk, k32_s[t, h], fac_s[t, h, 1:2]).astype(BF)

    def back_term(t):
        dn = mm(w_ref[...], dp_s[t])
        rr = rr_s[t]
        n32 = full[slot(2, t)].reshape(feat, toks).astype(F32) * rr
        part[1, t] = norm_back(dn, n32, rr).astype(BF).reshape(2, YS, 32, toks)

    def weight_terms(t):
        g = full[slot(1, t)].reshape(feat, toks)
        gq = mm_nt(nt_s[t], dp_s[t])
        go = mm_nt(mix_s[t], g)
        if t == 0:
            gq_ref[...] = gq
            go_ref[...] = go
        else:
            gq_ref[...] += gq
            go_ref[...] += go

    def backward(t):
        for h in range(heads):
            back_head(t, h)
        back_term(t)

    for load in loads[:3]:
        load.wait()
    pl.semaphore_wait(barrier, len(partners))

    order = [slot(2, 0), slot(1, 0), slot(0, 0)]
    across = {}
    for b in order + [slot(2, 1), slot(2, 2)]:
        across[b] = send(full.at[b, z, y], full.at[b, z, y], z_dev)
    mine = [Gather(b, z) for b in order]
    others = [Gather(b, 1 - z) for b in order]
    for g in mine:
        g.start()
    for load in loads[3:]:
        load.wait()
    wt[...] = w_ref[...].T
    wot[...] = wo_ref[...].T
    for g in mine:
        g.mid()
    make_mask(blab_ref, s, maskb, 0)
    make_mask(flab_ref, sections - 1 - s, maskf, 0)
    for b, g in zip(order, others):
        across[b].wait_recv()
        g.start()
    for t in range(1, TICKS):
        make_mask(blab_ref, t + s, maskb, t)
        make_mask(flab_ref, t - s + sections - 1, maskf, t)
    for g in mine:
        g.finish()
    for g in others:
        g.mid()
    others[0].finish()
    recompute(0)
    others[1].finish()

    for t in range(TICKS):
        last = t + 1 == TICKS
        if t > 0:
            old_f, old_b = chain_f, chain_b
            old_b.gather_finish()
        backward(t)
        chain_f, chain_b = Chain(0, t), Chain(1, t)
        chain_b.reduce_start()
        if t == 0:
            others[2].finish()
        else:
            old_f.gather_finish()
        forward(t)
        chain_f.reduce_start()
        weight_terms(t)
        chain_b.reduce_mid()
        chain_f.reduce_mid()
        chain_b.hand_over()
        chain_f.hand_over()
        if not last:
            across[slot(2, t + 1)].wait_recv()
            kept = [Gather(slot(2, t + 1), h) for h in range(2)]
            for g in kept:
                g.start()
            chain_b.gather_start()
            chain_f.gather_start()
            for g in kept:
                g.mid()
            chain_b.gather_mid()
            chain_f.gather_mid()
            for g in kept:
                g.finish()
            recompute(t + 1)

    for c, t, copy in outs:
        copy.wait_recv()
        out_ref[c, t] = (qown[c, t, z].astype(F32) + qrecv[c, t].astype(F32)).astype(BF)
    for c in copies:
        c.wait_send()


def hand_out(out_ref, gq_ref, go_ref, codes, grads, gq, go, out_v, gq_v, go_v, sems):
    rows = gq.shape[0] // 4
    moves = [(gq_ref.at[part], gq_v.at[part], gq.at[part]) for part in (pl.ds(rows * i, rows) for i in range(4))]
    moves.append((go_ref, go_v, go))
    moves += [(out_ref.at[i], out_v.at[i], out) for i, out in enumerate((codes, grads))]
    loads = [pltpu.make_async_copy(a, b, sems.at[0, i]) for i, (a, b, _) in enumerate(moves)]
    stores = [pltpu.make_async_copy(b, c, sems.at[1, i]) for i, (_, b, c) in enumerate(moves)]
    for c in loads:
        c.start()
    for load, store in zip(loads, stores):
        load.wait()
        store.start()
    for c in stores:
        c.wait()


def body(
    transit_latents,
    encoded_arrivals,
    arriving_latent_derivative,
    objective_derivative_arrivals,
    kept_inputs,
    onward_sequence_labels,
    reverse_sequence_labels,
    expander_attn_factors,
    outgoing_compressor_factors,
):
    sections = lax.axis_size("section")
    w, wo = jax.ShapeDtypeStruct(expander_attn_factors.shape[1:], BF), jax.ShapeDtypeStruct(outgoing_compressor_factors.shape[1:], BF)
    feat, cols = w.shape
    heads = cols // (3 * HD)
    toks, shard = transit_latents.shape[1:]
    vm = pl.BlockSpec(memory_space=pltpu.VMEM)
    block = (2, YS, shard, toks)
    hbm = pl.BlockSpec(memory_space=pl.ANY)
    scratch = [
        pltpu.VMEM((2, TICKS - 1, shard, toks), BF),
        pltpu.VMEM(onward_sequence_labels.shape, jnp.int32),
        pltpu.VMEM(reverse_sequence_labels.shape, jnp.int32),
        pltpu.VMEM((feat, cols), BF),
        pltpu.VMEM((heads * HD, feat), BF),
        pltpu.VMEM((3 * TICKS,) + block, BF),
        pltpu.VMEM((2, TICKS) + block, BF),
        pltpu.VMEM((2, TICKS, 2, 2, 4, shard, toks), BF),
        pltpu.VMEM((2, TICKS, 2, 2, shard, toks), BF),
        pltpu.VMEM((2, TICKS, 2, shard, toks), BF),
        pltpu.VMEM((2, TICKS, 2, shard, toks), BF),
        pltpu.VMEM((2, TICKS, shard, toks), BF),
        pltpu.VMEM((cols, feat), BF),
        pltpu.VMEM((feat, heads * HD), BF),
        pltpu.VMEM((TICKS, toks, toks), F32),
        pltpu.VMEM((TICKS, toks, toks), F32),
        pltpu.VMEM((TICKS, feat, toks), BF),
        pltpu.VMEM((TICKS, heads, HD, toks), F32),
        pltpu.VMEM((TICKS, heads, HD, toks), BF),
        pltpu.VMEM((TICKS, heads, HD, toks), BF),
        pltpu.VMEM((TICKS, heads, HD, toks), F32),
        pltpu.VMEM((TICKS, heads, toks, HD), BF),
        pltpu.VMEM((TICKS, heads, toks, toks), F32),
        pltpu.VMEM((TICKS, heads, toks, toks), BF),
        pltpu.VMEM((TICKS, heads * HD, toks), BF),
        pltpu.VMEM((TICKS, heads, 8, toks), F32),
        pltpu.VMEM((TICKS, 1, toks), F32),
        pltpu.VMEM((TICKS, cols, toks), BF),
        pltpu.SemaphoreType.DMA((9,)),
        pltpu.SemaphoreType.DMA((COPIES,)),
        pltpu.SemaphoreType.DMA((COPIES,)),
    ]
    out, gq, go = pl.pallas_call(
        functools.partial(kernel, sections),
        out_shape=(
            jax.ShapeDtypeStruct((2, TICKS, shard, toks), BF),
            jax.ShapeDtypeStruct(w.shape, F32),
            jax.ShapeDtypeStruct(wo.shape, F32),
        ),
        in_specs=[hbm] * 9,
        out_specs=(vm, vm, vm),
        scratch_shapes=scratch,
        compiler_params=pltpu.CompilerParams(
            collective_id=0, has_side_effects=True, vmem_limit_bytes=60 * 1024 * 1024
        ),
    )(
        transit_latents.swapaxes(1, 2),
        encoded_arrivals.swapaxes(1, 2),
        arriving_latent_derivative.swapaxes(1, 2),
        objective_derivative_arrivals.swapaxes(1, 2),
        kept_inputs.swapaxes(2, 3),
        onward_sequence_labels,
        reverse_sequence_labels,
        expander_attn_factors,
        outgoing_compressor_factors,
    )
    codes, grads, gq, go = pl.pallas_call(
        hand_out,
        out_shape=(
            jax.ShapeDtypeStruct(out.shape[1:], BF),
            jax.ShapeDtypeStruct(out.shape[1:], BF),
            jax.ShapeDtypeStruct(gq.shape, F32),
            jax.ShapeDtypeStruct(go.shape, F32),
        ),
        in_specs=[hbm] * 3,
        out_specs=[hbm] * 4,
        scratch_shapes=[
            pltpu.VMEM(out.shape, BF),
            pltpu.VMEM(gq.shape, F32),
            pltpu.VMEM(go.shape, F32),
            pltpu.SemaphoreType.DMA((2, 7)),
        ],
        compiler_params=pltpu.CompilerParams(vmem_limit_bytes=60 * 1024 * 1024),
    )(out, gq, go)
    return codes.swapaxes(1, 2)[None], grads.swapaxes(1, 2)[None], gq[None], go[None]


def solution(mesh):
    in_specs = (
        P("section", None, "tensor"),
        P(None, None, "tensor"),
        P("section", None, "tensor"),
        P(None, None, "tensor"),
        P("section", None, None, "tensor"),
        P(),
        P(),
        P("section", None, "tensor"),
        P("section", "tensor", None),
    )
    out_specs = (
        P("section", None, None, "tensor"),
        P("section", None, None, "tensor"),
        P("section", None, "tensor"),
        P("section", "tensor", None),
    )
    return jax.shard_map(body, mesh=mesh, in_specs=in_specs, out_specs=out_specs, check_vma=False)
```

```python
import functools

import jax
import jax.numpy as jnp
from jax import lax
from jax.experimental import pallas as pl
from jax.experimental.pallas import tpu as pltpu
from jax.sharding import PartitionSpec as P

HD = 128
SCALE = 8.0 / 128
NORM_EPS = 1e-05
HEAD_EPS = 1e-06
TICKS = 3
YS = 8
COPIES = 268
POOL = 64
BF = jnp.bfloat16
F32 = jnp.float32


def mm(a, b):
    return jnp.dot(a, b, preferred_element_type=F32)


def mm_nt(a, b):
    return lax.dot_general(a, b, (((1,), (1,)), ((), ())), preferred_element_type=F32)


def kernel(
    sections,
    codes_hbm, feed_hbm, grad_hbm, loss_hbm, kept_hbm, flab_hbm, blab_hbm, w_hbm, wo_hbm,
    out_ref, gq_ref, go_ref,
    enter, flab_ref, blab_ref, w_ref, wo_ref,
    full, part, rsb, zbuf, qsend, qown, qrecv,
    wt, wot, maskf, maskb,
    nt_s, q32_s, qn_s, kn_s, k32_s, v_s, p_s, pb_s, mix_s, fac_s, rr_s, dp_s,
    load_sems, send_sems, recv_sems,
):
    feat, toks = 512, 256
    heads = w_ref.shape[1] // (3 * HD)
    s = lax.axis_index("section")
    rank = lax.axis_index("tensor")
    z = rank // YS
    y = rank % YS

    def at(k):
        return (y + k + YS) % YS

    nxt, prv = (s + 1) % sections, (s + sections - 1) % sections

    def dev(sec, zz, yy):
        return {"section": sec, "tensor": zz * YS + yy}

    ring = {k: dev(s, z, at(k)) for k in (1, -1, 2, -2)}
    z_dev = dev(s, 1 - z, y)
    partners = (*ring.values(), z_dev, dev(nxt, z, y), dev(nxt, 1 - z, y), dev(prv, z, y), dev(prv, 1 - z, y))
    barrier = pltpu.get_barrier_semaphore()
    for p in partners:
        pl.semaphore_signal(barrier, inc=1, device_id=p, device_id_type=pl.DeviceIdType.MESH)

    loads = []
    for src, dst in (
        (kept_hbm.at[0], full.at[pl.ds(2 * TICKS, TICKS), z, y]),
        (grad_hbm, full.at[pl.ds(TICKS, 1), z, y]),
        (codes_hbm, full.at[pl.ds(0, 1), z, y]),
        (w_hbm.at[0], w_ref),
        (wo_hbm.at[0], wo_ref),
        (blab_hbm, blab_ref),
        (flab_hbm, flab_ref),
        (feed_hbm, enter.at[0]),
        (loss_hbm, enter.at[1]),
    ):
        load = pltpu.make_async_copy(src, dst, load_sems.at[len(loads)])
        load.start()
        loads.append(load)

    copies = []
    drained = [0]

    def drain(count):
        for c in copies[drained[0]:count]:
            c.wait_send()
        drained[0] = count

    def send(src, dst, target):
        i = len(copies)
        drain(max(drained[0], i - POOL + 1))
        c = pltpu.make_async_remote_copy(
            src_ref=src, dst_ref=dst, send_sem=send_sems.at[i % POOL], recv_sem=recv_sems.at[i],
            device_id=target, device_id_type=pl.DeviceIdType.MESH,
        )
        c.start()
        copies.append(c)
        return c

    class Gather:
        def __init__(self, b, h):
            self.block = lambda k: full.at[b, h, at(k)]
            self.parts = lambda k, i: full.at[b, h, at(k), pl.ds(16 * i, 16)]

        def start(self):
            own = self.block(0)
            self.two = [send(own, own, ring[2]), send(own, own, ring[-2])]
            self.rest = [send(own, own, ring[1]), send(own, own, ring[-1])]

        def mid(self):
            for i, d in enumerate((1, -1)):
                self.two[i].wait_recv()
                far = self.parts(-2 * d, i)
                self.rest.append(send(far, far, ring[2 * d]))
                block = self.block(-2 * d)
                self.rest.append(send(block, block, ring[d]))

        def finish(self):
            for c in self.rest:
                c.wait_recv()

    class Reduce:
        def __init__(self, c, t, h):
            self.h = h
            self.p = part.at[c, t, h]
            self.r = rsb.at[c, t, h]

        def start(self):
            p, r = self.p, self.r
            self.first = []
            for i, d in enumerate((1, -1)):
                rows = pl.ds(16 * i, 16)
                far = send(p.at[at(4 * d), rows], r.at[i, 1, rows], ring[2 * d])
                self.first.append((far, send(p.at[at(3 * d)], r.at[i, 0], ring[d])))
            self.rest = [send(p.at[at(d)], r.at[i, 3], ring[d]) for i, d in enumerate((1, -1))]

        def mid(self):
            p, r = self.p, self.r
            for i, d in enumerate((1, -1)):
                for c in self.first[i]:
                    c.wait_recv()
                both = r[i, 0].astype(F32) + p[at(2 * d)].astype(F32)
                far = r[i, 1, 16 * i:16 * i + 16].astype(F32)
                none = jnp.zeros_like(far)
                both = both + jnp.concatenate([far, none] if i == 0 else [none, far], axis=0)
                r[i, 0] = both.astype(BF)
                self.rest.append(send(r.at[i, 0], r.at[i, 2], ring[2 * d]))

        def finish(self):
            for c in self.rest:
                c.wait_recv()
            r = self.r
            total = self.p[y].astype(F32)
            for i in range(2):
                total = total + r[i, 2].astype(F32) + r[i, 3].astype(F32)
            return total

    outs = []

    class Pass:
        def __init__(self, c, t, h):
            self.c, self.t, self.h = c, t, h

        def start(self, total, b):
            c, t, h = self.c, self.t, self.h
            none = jnp.zeros((32, toks), F32)
            rows = (total + jnp.where(z == h, full[b, h, y].astype(F32), none)).astype(BF)
            qown[c, t, h] = rows
            if t + 1 < TICKS:
                edge = (s == sections - 1) if c == 0 else (s == 0)
                entering = jnp.where(z == h, enter[c, t], none.astype(BF))
                qsend[c, t, h] = jnp.where(edge, entering, rows)
                to = nxt if c == 0 else prv
                self.far = send(qsend.at[c, t, h], zbuf.at[c, t, 1, h], dev(to, 1 - z, y))
                self.near = send(qsend.at[c, t, h], zbuf.at[c, t, 0, h], dev(to, z, y))

        def arrive(self, b):
            self.near.wait_recv()
            self.far.wait_recv()
            c, t, h = self.c, self.t, self.h
            full[b, h, y] = (zbuf[c, t, 0, h].astype(F32) + zbuf[c, t, 1, h].astype(F32)).astype(BF)

    class Chain:
        def __init__(self, c, t):
            self.c, self.t = c, t
            self.halves = (0, 1) if t + 1 < TICKS else (1 - z, z)
            self.reduces = [Reduce(c, t, h) for h in self.halves]
            self.passes = [Pass(c, t, h) for h in self.halves]
            self.gathers = [Gather(slot(c, t + 1), h) for h in self.halves]

        def reduce_start(self):
            for r in self.reduces:
                r.start()

        def reduce_mid(self):
            for r in self.reduces:
                r.mid()

        def hand_over(self):
            c, t = self.c, self.t
            for i in range(2):
                self.passes[i].start(self.reduces[i].finish(), slot(c, t))
                if i == 0 and t + 1 == TICKS:
                    self.swap()

        def swap(self):
            c, t = self.c, self.t
            outs.append((c, t, send(qown.at[c, t, 1 - z], qrecv.at[c, t], z_dev)))

        def gather_start(self):
            for i in range(2):
                self.passes[i].arrive(slot(self.c, self.t + 1))
                self.gathers[i].start()

        def gather_mid(self):
            for g in self.gathers:
                g.mid()

        def gather_finish(self):
            for g in self.gathers:
                g.finish()

    def slot(kind, t):
        return kind * TICKS + t

    def make_mask(ref, row, out, t):
        seg = jnp.broadcast_to(ref[pl.ds(row, 1), :].astype(F32), (toks, toks))
        segt = seg.T
        j = lax.broadcasted_iota(jnp.int32, (toks, toks), 0)
        i = lax.broadcasted_iota(jnp.int32, (toks, toks), 1)
        out[t] = jnp.where((j <= i) & (seg == segt), 1.0, 0.0)

    def normed(b):
        a = full[b].reshape(feat, toks).astype(F32)
        rr = lax.rsqrt(jnp.mean(a * a, axis=0, keepdims=True) + NORM_EPS)
        return a * rr, rr

    def head_norm(x):
        f = lax.rsqrt(jnp.mean(x * x, axis=0, keepdims=True) + HEAD_EPS)
        return x * f, f

    def probs(qn, kn, mask):
        w = jnp.exp(mm(kn, qn) * SCALE) * mask
        return w * (1.0 / jnp.sum(w, axis=0, keepdims=True))

    def forward(t):
        n32, _ = normed(slot(0, t))
        packed = mm(wt[...], n32.astype(BF)).astype(BF)
        mask = maskf[t]
        hs = range(heads)
        rows = [[packed[3 * HD * h + HD * i:3 * HD * h + HD * (i + 1)] for i in range(3)] for h in hs]
        qn = [head_norm(rows[h][0].astype(F32))[0].astype(BF) for h in hs]
        kn = [head_norm(rows[h][1].astype(F32))[0].astype(BF).T for h in hs]
        w = [jnp.exp(mm(kn[h], qn[h]) * SCALE) * mask for h in hs]
        p = [(w[h] * (1.0 / jnp.sum(w[h], axis=0, keepdims=True))).astype(BF) for h in hs]
        mixed = [mm(rows[h][2], p[h]).astype(BF) for h in hs]
        term = mm(wot[...], jnp.concatenate(mixed, axis=0))
        part[0, t] = term.astype(BF).reshape(2, YS, 32, toks)

    def recompute(t):
        n32, rr = normed(slot(2, t))
        n = n32.astype(BF)
        nt_s[t] = n
        rr_s[t] = rr
        packed = mm(wt[...], n).astype(BF)
        mask = maskb[t]
        for h in range(heads):
            base = 3 * HD * h
            q32, sq = head_norm(packed[base:base + HD].astype(F32))
            k32, sk = head_norm(packed[base + HD:base + 2 * HD].astype(F32))
            v = packed[base + 2 * HD:base + 3 * HD]
            q32_s[t, h], k32_s[t, h] = q32, k32
            fac_s[t, h, 0:1], fac_s[t, h, 1:2] = sq, sk
            qn, kn = q32.astype(BF), k32.astype(BF)
            qn_s[t, h], kn_s[t, h] = qn, kn
            v_s[t, h] = v.T
            p = probs(qn, kn.T, mask)
            p_s[t, h] = p
            pb = p.astype(BF)
            pb_s[t, h] = pb
            mix_s[t, h * HD:(h + 1) * HD] = mm(v, pb).astype(BF)

    def norm_back(grad, unit, factor):
        return factor * (grad - unit * jnp.mean(grad * unit, axis=0, keepdims=True))

    def back_heads(t):
        hs = range(heads)
        g = full[slot(1, t)].reshape(feat, toks)
        dm = mm(wo_ref[...], g).astype(BF)
        dm = [dm[h * HD:(h + 1) * HD] for h in hs]
        dp = [mm(v_s[t, h], dm[h]) for h in hs]
        pd = [p_s[t, h] * dp[h] for h in hs]
        inner = [jnp.sum(pd[h], axis=0, keepdims=True) for h in hs]
        ds = [((pd[h] - p_s[t, h] * inner[h]) * SCALE).astype(BF) for h in hs]
        dv = [mm_nt(dm[h], pb_s[t, h]) for h in hs]
        dq = [mm(kn_s[t, h], ds[h]) for h in hs]
        dk = [mm_nt(qn_s[t, h], ds[h]) for h in hs]
        for h in hs:
            base = 3 * HD * h
            dp_s[t, base + 2 * HD:base + 3 * HD] = dv[h].astype(BF)
            dp_s[t, base:base + HD] = norm_back(dq[h], q32_s[t, h], fac_s[t, h, 0:1]).astype(BF)
            dp_s[t, base + HD:base + 2 * HD] = norm_back(dk[h], k32_s[t, h], fac_s[t, h, 1:2]).astype(BF)

    def back_term(t):
        dn = mm(w_ref[...], dp_s[t])
        rr = rr_s[t]
        n32 = full[slot(2, t)].reshape(feat, toks).astype(F32) * rr
        part[1, t] = norm_back(dn, n32, rr).astype(BF).reshape(2, YS, 32, toks)

    def weight_terms(t):
        g = full[slot(1, t)].reshape(feat, toks)
        gq = mm_nt(nt_s[t], dp_s[t])
        go = mm_nt(mix_s[t], g)
        if t == 0:
            gq_ref[...] = gq
            go_ref[...] = go
        else:
            gq_ref[...] += gq
            go_ref[...] += go

    def backward(t):
        back_heads(t)
        back_term(t)

    for load in loads[:3]:
        load.wait()
    pl.semaphore_wait(barrier, len(partners))

    order = [slot(0, 0), slot(2, 0), slot(1, 0)]
    across = {}
    for b in order + [slot(2, 1), slot(2, 2)]:
        across[b] = send(full.at[b, z, y], full.at[b, z, y], z_dev)
    mine = [Gather(b, z) for b in order]
    others = [Gather(b, 1 - z) for b in order]
    for g in mine:
        g.start()
    for load in loads[3:]:
        load.wait()
    wt[...] = w_ref[...].T
    wot[...] = wo_ref[...].T
    for g in mine:
        g.mid()
    make_mask(blab_ref, s, maskb, 0)
    make_mask(flab_ref, sections - 1 - s, maskf, 0)
    for b, g in zip(order, others):
        across[b].wait_recv()
        g.start()
    for t in range(1, TICKS):
        make_mask(blab_ref, t + s, maskb, t)
        make_mask(flab_ref, t - s + sections - 1, maskf, t)
    for g in mine:
        g.finish()
    for g in others:
        g.mid()

    for t in range(TICKS):
        last = t + 1 == TICKS
        if t > 0:
            old_f, old_b = chain_f, chain_b
            old_f.gather_finish()
            forward(t)
        chain_f, chain_b = Chain(0, t), Chain(1, t)
        count = len(copies)
        if t == 0:
            others[0].finish()
            forward(0)
            chain_f.reduce_start()
            others[1].finish()
            recompute(0)
            others[2].finish()
        else:
            chain_f.reduce_start()
            old_b.gather_finish()
        backward(t)
        chain_b.reduce_start()
        weight_terms(t)
        drain(count)
        chain_f.reduce_mid()
        chain_b.reduce_mid()
        count = len(copies)
        chain_f.hand_over()
        chain_b.hand_over()
        if not last:
            across[slot(2, t + 1)].wait_recv()
            kept = [Gather(slot(2, t + 1), h) for h in range(2)]
            for g in kept:
                g.start()
        drain(count)
        if not last:
            chain_f.gather_start()
            chain_b.gather_start()
            chain_f.swap()
            chain_b.swap()
            for g in kept:
                g.mid()
            chain_f.gather_mid()
            chain_b.gather_mid()
            for g in kept:
                g.finish()
            recompute(t + 1)

    for c, t, copy in outs:
        copy.wait_recv()
        out_ref[c, t] = (qown[c, t, z].astype(F32) + qrecv[c, t].astype(F32)).astype(BF)
    drain(len(copies))


def hand_out(out_ref, gq_ref, go_ref, codes, grads, gq, go, out_v, gq_v, go_v, sems):
    rows = gq.shape[0] // 4
    moves = [(gq_ref.at[part], gq_v.at[part], gq.at[part]) for part in (pl.ds(rows * i, rows) for i in range(4))]
    moves.append((go_ref, go_v, go))
    moves += [(out_ref.at[i], out_v.at[i], out) for i, out in enumerate((codes, grads))]
    loads = [pltpu.make_async_copy(a, b, sems.at[0, i]) for i, (a, b, _) in enumerate(moves)]
    stores = [pltpu.make_async_copy(b, c, sems.at[1, i]) for i, (_, b, c) in enumerate(moves)]
    for c in loads:
        c.start()
    for load, store in zip(loads, stores):
        load.wait()
        store.start()
    for c in stores:
        c.wait()


def body(
    transit_latents,
    encoded_arrivals,
    arriving_latent_derivative,
    objective_derivative_arrivals,
    kept_inputs,
    onward_sequence_labels,
    reverse_sequence_labels,
    expander_attn_factors,
    outgoing_compressor_factors,
):
    sections = lax.axis_size("section")
    w, wo = jax.ShapeDtypeStruct(expander_attn_factors.shape[1:], BF), jax.ShapeDtypeStruct(outgoing_compressor_factors.shape[1:], BF)
    feat, cols = w.shape
    heads = cols // (3 * HD)
    toks, shard = transit_latents.shape[1:]
    vm = pl.BlockSpec(memory_space=pltpu.VMEM)
    block = (2, YS, shard, toks)
    hbm = pl.BlockSpec(memory_space=pl.ANY)
    scratch = [
        pltpu.VMEM((2, TICKS - 1, shard, toks), BF),
        pltpu.VMEM(onward_sequence_labels.shape, jnp.int32),
        pltpu.VMEM(reverse_sequence_labels.shape, jnp.int32),
        pltpu.VMEM((feat, cols), BF),
        pltpu.VMEM((heads * HD, feat), BF),
        pltpu.VMEM((3 * TICKS,) + block, BF),
        pltpu.VMEM((2, TICKS) + block, BF),
        pltpu.VMEM((2, TICKS, 2, 2, 4, shard, toks), BF),
        pltpu.VMEM((2, TICKS, 2, 2, shard, toks), BF),
        pltpu.VMEM((2, TICKS, 2, shard, toks), BF),
        pltpu.VMEM((2, TICKS, 2, shard, toks), BF),
        pltpu.VMEM((2, TICKS, shard, toks), BF),
        pltpu.VMEM((cols, feat), BF),
        pltpu.VMEM((feat, heads * HD), BF),
        pltpu.VMEM((TICKS, toks, toks), F32),
        pltpu.VMEM((TICKS, toks, toks), F32),
        pltpu.VMEM((TICKS, feat, toks), BF),
        pltpu.VMEM((TICKS, heads, HD, toks), F32),
        pltpu.VMEM((TICKS, heads, HD, toks), BF),
        pltpu.VMEM((TICKS, heads, HD, toks), BF),
        pltpu.VMEM((TICKS, heads, HD, toks), F32),
        pltpu.VMEM((TICKS, heads, toks, HD), BF),
        pltpu.VMEM((TICKS, heads, toks, toks), F32),
        pltpu.VMEM((TICKS, heads, toks, toks), BF),
        pltpu.VMEM((TICKS, heads * HD, toks), BF),
        pltpu.VMEM((TICKS, heads, 8, toks), F32),
        pltpu.VMEM((TICKS, 1, toks), F32),
        pltpu.VMEM((TICKS, cols, toks), BF),
        pltpu.SemaphoreType.DMA((9,)),
        pltpu.SemaphoreType.DMA((POOL,)),
        pltpu.SemaphoreType.DMA((COPIES,)),
    ]
    out, gq, go = pl.pallas_call(
        functools.partial(kernel, sections),
        out_shape=(
            jax.ShapeDtypeStruct((2, TICKS, shard, toks), BF),
            jax.ShapeDtypeStruct(w.shape, F32),
            jax.ShapeDtypeStruct(wo.shape, F32),
        ),
        in_specs=[hbm] * 9,
        out_specs=(vm, vm, vm),
        scratch_shapes=scratch,
        compiler_params=pltpu.CompilerParams(
            collective_id=0, has_side_effects=True, vmem_limit_bytes=60 * 1024 * 1024
        ),
    )(
        transit_latents.swapaxes(1, 2),
        encoded_arrivals.swapaxes(1, 2),
        arriving_latent_derivative.swapaxes(1, 2),
        objective_derivative_arrivals.swapaxes(1, 2),
        kept_inputs.swapaxes(2, 3),
        onward_sequence_labels,
        reverse_sequence_labels,
        expander_attn_factors,
        outgoing_compressor_factors,
    )
    codes, grads, gq, go = pl.pallas_call(
        hand_out,
        out_shape=(
            jax.ShapeDtypeStruct(out.shape[1:], BF),
            jax.ShapeDtypeStruct(out.shape[1:], BF),
            jax.ShapeDtypeStruct(gq.shape, F32),
            jax.ShapeDtypeStruct(go.shape, F32),
        ),
        in_specs=[hbm] * 3,
        out_specs=[hbm] * 4,
        scratch_shapes=[
            pltpu.VMEM(out.shape, BF),
            pltpu.VMEM(gq.shape, F32),
            pltpu.VMEM(go.shape, F32),
            pltpu.SemaphoreType.DMA((2, 7)),
        ],
        compiler_params=pltpu.CompilerParams(vmem_limit_bytes=60 * 1024 * 1024),
    )(out, gq, go)
    return codes.swapaxes(1, 2)[None], grads.swapaxes(1, 2)[None], gq[None], go[None]


def solution(mesh):
    in_specs = (
        P("section", None, "tensor"),
        P(None, None, "tensor"),
        P("section", None, "tensor"),
        P(None, None, "tensor"),
        P("section", None, None, "tensor"),
        P(),
        P(),
        P("section", None, "tensor"),
        P("section", "tensor", None),
    )
    out_specs = (
        P("section", None, None, "tensor"),
        P("section", None, None, "tensor"),
        P("section", None, "tensor"),
        P("section", "tensor", None),
    )
    return jax.shard_map(body, mesh=mesh, in_specs=in_specs, out_specs=out_specs, check_vma=False)
```

```python
import functools

import jax
import jax.numpy as jnp
from jax import lax
from jax.experimental import pallas as pl
from jax.experimental.pallas import tpu as pltpu
from jax.sharding import PartitionSpec as P

HD = 128
SCALE = 8.0 / 128
NORM_EPS = 1e-05
HEAD_EPS = 1e-06
TICKS = 3
YS = 8
COPIES = 108
POOL = 64
BF = jnp.bfloat16
F32 = jnp.float32


def mm(a, b):
    return jnp.dot(a, b, preferred_element_type=F32)


def mm_nt(a, b):
    return lax.dot_general(a, b, (((1,), (1,)), ((), ())), preferred_element_type=F32)


def kernel(
    sections,
    codes_hbm, feed_hbm, grad_hbm, loss_hbm, kept_hbm, flab_hbm, blab_hbm, w_hbm, wo_hbm,
    out_ref, gq_ref, go_ref,
    enter, flab_ref, blab_ref, w_ref, wo_ref,
    full, part, rsb, zbuf, qsend, qown, qrecv,
    wt, wot, maskf, maskb,
    nt_s, q32_s, qn_s, kn_s, k32_s, v_s, p_s, pb_s, mix_s, fac_s, rr_s, dp_s,
    load_sems, send_sems, recv_sems,
):
    feat, toks = 512, 256
    heads = w_ref.shape[1] // (3 * HD)
    s = lax.axis_index("section")
    rank = lax.axis_index("tensor")
    z = rank // YS
    y = rank % YS

    def at(k):
        return (y + k + YS) % YS

    nxt, prv = (s + 1) % sections, (s + sections - 1) % sections

    def dev(sec, zz, yy):
        return {"section": sec, "tensor": zz * YS + yy}

    ring = {k: dev(s, z, at(k)) for k in (1, -1, 2, -2)}
    z_dev = dev(s, 1 - z, y)
    partners = (*ring.values(), z_dev, dev(nxt, z, y), dev(nxt, 1 - z, y), dev(prv, z, y), dev(prv, 1 - z, y))
    barrier = pltpu.get_barrier_semaphore()
    for p in partners:
        pl.semaphore_signal(barrier, inc=1, device_id=p, device_id_type=pl.DeviceIdType.MESH)

    loads = []
    for src, dst in (
        (kept_hbm.at[0], full.at[pl.ds(2 * TICKS, TICKS), z, y]),
        (grad_hbm, full.at[pl.ds(TICKS, 1), z, y]),
        (codes_hbm, full.at[pl.ds(0, 1), z, y]),
        (w_hbm.at[0], w_ref),
        (wo_hbm.at[0], wo_ref),
        (blab_hbm, blab_ref),
        (flab_hbm, flab_ref),
        (feed_hbm, enter.at[0]),
        (loss_hbm, enter.at[1]),
    ):
        load = pltpu.make_async_copy(src, dst, load_sems.at[len(loads)])
        load.start()
        loads.append(load)

    copies = []
    drained = [0]

    def drain(count):
        for c in copies[drained[0]:count]:
            c.wait_send()
        drained[0] = count

    single = [80]

    def send(src, dst, target, base=None):
        i = len(copies)
        if base is None:
            arrival = single[0]
            single[0] += 1
        else:
            arrival = base[0]
            base[0] += 1
        drain(max(drained[0], i - POOL + 1))
        c = pltpu.make_async_remote_copy(
            src_ref=src, dst_ref=dst, send_sem=send_sems.at[i % POOL], recv_sem=recv_sems.at[arrival],
            device_id=target, device_id_type=pl.DeviceIdType.MESH,
        )
        c.start()
        copies.append(c)
        return c

    class Gather:
        def __init__(self, b, h, base):
            self.base = [base]
            self.block = lambda k: full.at[b, h, at(k)]
            self.parts = lambda k, i: full.at[b, h, at(k), pl.ds(16 * i, 16)]

        def start(self):
            own = self.block(0)
            self.two = [send(own, own, ring[2], self.base), send(own, own, ring[-2], self.base)]
            self.rest = [send(own, own, ring[1], self.base), send(own, own, ring[-1], self.base)]

        def mid(self):
            for i, d in enumerate((1, -1)):
                self.two[i].wait_recv()
                far = self.parts(-2 * d, i)
                self.rest.append(send(far, far, ring[2 * d], self.base))
                block = self.block(-2 * d)
                self.rest.append(send(block, block, ring[d], self.base))

        def finish(self):
            for c in self.rest:
                c.wait_recv()

    class Reduce:
        def __init__(self, c, t, h, base):
            self.base = [base]
            self.p = part.at[c, t, h]
            self.r = rsb.at[c, t, h]

        def start(self):
            p, r = self.p, self.r
            self.first = []
            for i, d in enumerate((1, -1)):
                rows = pl.ds(16 * i, 16)
                far = send(p.at[at(4 * d), rows], r.at[i, 1, rows], ring[2 * d], self.base)
                self.first.append((far, send(p.at[at(3 * d)], r.at[i, 0], ring[d], self.base)))
            self.rest = [send(p.at[at(d)], r.at[i, 3], ring[d], self.base) for i, d in enumerate((1, -1))]

        def mid(self):
            p, r = self.p, self.r
            for i, d in enumerate((1, -1)):
                for c in self.first[i]:
                    c.wait_recv()
                both = r[i, 0].astype(F32) + p[at(2 * d)].astype(F32)
                far = r[i, 1, 16 * i:16 * i + 16].astype(F32)
                none = jnp.zeros_like(far)
                both = both + jnp.concatenate([far, none] if i == 0 else [none, far], axis=0)
                r[i, 0] = both.astype(BF)
                self.rest.append(send(r.at[i, 0], r.at[i, 2], ring[2 * d], self.base))

        def finish(self):
            for c in self.rest:
                c.wait_recv()
            r = self.r
            total = self.p[y].astype(F32)
            for i in range(2):
                total = total + r[i, 2].astype(F32) + r[i, 3].astype(F32)
            return total

    outs = []

    class Pass:
        def __init__(self, c, t, h):
            self.c, self.t, self.h = c, t, h

        def start(self, total, b):
            c, t, h = self.c, self.t, self.h
            none = jnp.zeros((32, toks), F32)
            rows = (total + jnp.where(z == h, full[b, h, y].astype(F32), none)).astype(BF)
            qown[c, t, h] = rows
            if t + 1 < TICKS:
                edge = (s == sections - 1) if c == 0 else (s == 0)
                entering = jnp.where(z == h, enter[c, t], none.astype(BF))
                qsend[c, t, h] = jnp.where(edge, entering, rows)
                to = nxt if c == 0 else prv
                self.far = send(qsend.at[c, t, h], zbuf.at[c, t, 1, h], dev(to, 1 - z, y))
                self.near = send(qsend.at[c, t, h], zbuf.at[c, t, 0, h], dev(to, z, y))

        def arrive(self, b):
            self.near.wait_recv()
            self.far.wait_recv()
            c, t, h = self.c, self.t, self.h
            full[b, h, y] = (zbuf[c, t, 0, h].astype(F32) + zbuf[c, t, 1, h].astype(F32)).astype(BF)

    class Chain:
        def __init__(self, c, t):
            self.c, self.t = c, t
            self.halves = (0, 1) if t + 1 < TICKS else (1 - z, z)
            self.reduces = [Reduce(c, t, h, 48 + 16 * c + 8 * i) for i, h in enumerate(self.halves)]
            self.passes = [Pass(c, t, h) for h in self.halves]
            self.gathers = [Gather(slot(c, t + 1), h, 32 * c + 8 * i) for i, h in enumerate(self.halves)]

        def reduce_start(self):
            for r in self.reduces:
                r.start()

        def reduce_mid(self):
            for r in self.reduces:
                r.mid()

        def hand_over(self):
            c, t = self.c, self.t
            for i in range(2):
                self.passes[i].start(self.reduces[i].finish(), slot(c, t))
                if i == 0 and t + 1 == TICKS:
                    self.swap()

        def swap(self):
            c, t = self.c, self.t
            outs.append((c, t, send(qown.at[c, t, 1 - z], qrecv.at[c, t], z_dev)))

        def gather_start(self):
            for i in range(2):
                self.passes[i].arrive(slot(self.c, self.t + 1))
                self.gathers[i].start()

        def gather_mid(self):
            for g in self.gathers:
                g.mid()

        def gather_finish(self):
            for g in self.gathers:
                g.finish()

    def slot(kind, t):
        return kind * TICKS + t

    def make_mask(ref, row, out, t):
        seg = jnp.broadcast_to(ref[pl.ds(row, 1), :].astype(F32), (toks, toks))
        segt = seg.T
        j = lax.broadcasted_iota(jnp.int32, (toks, toks), 0)
        i = lax.broadcasted_iota(jnp.int32, (toks, toks), 1)
        out[t] = jnp.where((j <= i) & (seg == segt), 1.0, 0.0)

    def normed(b):
        a = full[b].reshape(feat, toks).astype(F32)
        rr = lax.rsqrt(jnp.mean(a * a, axis=0, keepdims=True) + NORM_EPS)
        return a * rr, rr

    def head_norm(x):
        f = lax.rsqrt(jnp.mean(x * x, axis=0, keepdims=True) + HEAD_EPS)
        return x * f, f

    def probs(qn, kn, mask):
        w = jnp.exp(mm(kn, qn) * SCALE) * mask
        return w * (1.0 / jnp.sum(w, axis=0, keepdims=True))

    def forward(t):
        n32, _ = normed(slot(0, t))
        packed = mm(wt[...], n32.astype(BF)).astype(BF)
        mask = maskf[t]
        hs = range(heads)
        rows = [[packed[3 * HD * h + HD * i:3 * HD * h + HD * (i + 1)] for i in range(3)] for h in hs]
        qn = [head_norm(rows[h][0].astype(F32))[0].astype(BF) for h in hs]
        kn = [head_norm(rows[h][1].astype(F32))[0].astype(BF).T for h in hs]
        w = [jnp.exp(mm(kn[h], qn[h]) * SCALE) * mask for h in hs]
        p = [(w[h] * (1.0 / jnp.sum(w[h], axis=0, keepdims=True))).astype(BF) for h in hs]
        mixed = [mm(rows[h][2], p[h]).astype(BF) for h in hs]
        term = mm(wot[...], jnp.concatenate(mixed, axis=0))
        part[0, t] = term.astype(BF).reshape(2, YS, 32, toks)

    def recompute(t):
        n32, rr = normed(slot(2, t))
        n = n32.astype(BF)
        nt_s[t] = n
        rr_s[t] = rr
        packed = mm(wt[...], n).astype(BF)
        mask = maskb[t]
        for h in range(heads):
            base = 3 * HD * h
            q32, sq = head_norm(packed[base:base + HD].astype(F32))
            k32, sk = head_norm(packed[base + HD:base + 2 * HD].astype(F32))
            v = packed[base + 2 * HD:base + 3 * HD]
            q32_s[t, h], k32_s[t, h] = q32, k32
            fac_s[t, h, 0:1], fac_s[t, h, 1:2] = sq, sk
            qn, kn = q32.astype(BF), k32.astype(BF)
            qn_s[t, h], kn_s[t, h] = qn, kn
            v_s[t, h] = v.T
            p = probs(qn, kn.T, mask)
            p_s[t, h] = p
            pb = p.astype(BF)
            pb_s[t, h] = pb
            mix_s[t, h * HD:(h + 1) * HD] = mm(v, pb).astype(BF)

    def norm_back(grad, unit, factor):
        return factor * (grad - unit * jnp.mean(grad * unit, axis=0, keepdims=True))

    def back_heads(t):
        hs = range(heads)
        g = full[slot(1, t)].reshape(feat, toks)
        dm = mm(wo_ref[...], g).astype(BF)
        dm = [dm[h * HD:(h + 1) * HD] for h in hs]
        dp = [mm(v_s[t, h], dm[h]) for h in hs]
        pd = [p_s[t, h] * dp[h] for h in hs]
        inner = [jnp.sum(pd[h], axis=0, keepdims=True) for h in hs]
        ds = [((pd[h] - p_s[t, h] * inner[h]) * SCALE).astype(BF) for h in hs]
        dv = [mm_nt(dm[h], pb_s[t, h]) for h in hs]
        dq = [mm(kn_s[t, h], ds[h]) for h in hs]
        dk = [mm_nt(qn_s[t, h], ds[h]) for h in hs]
        for h in hs:
            base = 3 * HD * h
            dp_s[t, base + 2 * HD:base + 3 * HD] = dv[h].astype(BF)
            dp_s[t, base:base + HD] = norm_back(dq[h], q32_s[t, h], fac_s[t, h, 0:1]).astype(BF)
            dp_s[t, base + HD:base + 2 * HD] = norm_back(dk[h], k32_s[t, h], fac_s[t, h, 1:2]).astype(BF)

    def back_term(t):
        dn = mm(w_ref[...], dp_s[t])
        rr = rr_s[t]
        n32 = full[slot(2, t)].reshape(feat, toks).astype(F32) * rr
        part[1, t] = norm_back(dn, n32, rr).astype(BF).reshape(2, YS, 32, toks)

    def weight_terms(t):
        g = full[slot(1, t)].reshape(feat, toks)
        gq = mm_nt(nt_s[t], dp_s[t])
        go = mm_nt(mix_s[t], g)
        if t == 0:
            gq_ref[...] = gq
            go_ref[...] = go
        else:
            gq_ref[...] += gq
            go_ref[...] += go

    def backward(t):
        back_heads(t)
        back_term(t)

    for load in loads[:3]:
        load.wait()
    pl.semaphore_wait(barrier, len(partners))

    order = [slot(0, 0), slot(2, 0), slot(1, 0)]
    across = {}
    for b in order + [slot(2, 1), slot(2, 2)]:
        across[b] = send(full.at[b, z, y], full.at[b, z, y], z_dev)
    mine = [Gather(b, z, 16 * i) for i, b in enumerate(order)]
    others = [Gather(b, 1 - z, 16 * i + 8) for i, b in enumerate(order)]
    for g in mine:
        g.start()
    for load in loads[3:]:
        load.wait()
    wt[...] = w_ref[...].T
    wot[...] = wo_ref[...].T
    for g in mine:
        g.mid()
    make_mask(blab_ref, s, maskb, 0)
    make_mask(flab_ref, sections - 1 - s, maskf, 0)
    for b, g in zip(order, others):
        across[b].wait_recv()
        g.start()
    for t in range(1, TICKS):
        make_mask(blab_ref, t + s, maskb, t)
        make_mask(flab_ref, t - s + sections - 1, maskf, t)
    for g in mine:
        g.finish()
    for g in others:
        g.mid()

    for t in range(TICKS):
        last = t + 1 == TICKS
        if t > 0:
            old_f, old_b = chain_f, chain_b
            old_f.gather_finish()
            forward(t)
        chain_f, chain_b = Chain(0, t), Chain(1, t)
        count = len(copies)
        if t == 0:
            others[0].finish()
            forward(0)
            chain_f.reduce_start()
            others[1].finish()
            recompute(0)
            others[2].finish()
        else:
            chain_f.reduce_start()
            old_b.gather_finish()
        backward(t)
        chain_b.reduce_start()
        weight_terms(t)
        drain(count)
        chain_f.reduce_mid()
        chain_b.reduce_mid()
        count = len(copies)
        chain_f.hand_over()
        chain_b.hand_over()
        if not last:
            across[slot(2, t + 1)].wait_recv()
            kept = [Gather(slot(2, t + 1), h, 16 + 8 * h) for h in range(2)]
            for g in kept:
                g.start()
        drain(count)
        if not last:
            chain_f.gather_start()
            chain_b.gather_start()
            chain_f.swap()
            chain_b.swap()
            for g in kept:
                g.mid()
            chain_f.gather_mid()
            chain_b.gather_mid()
            for g in kept:
                g.finish()
            recompute(t + 1)

    for c, t, copy in outs:
        copy.wait_recv()
        out_ref[c, t] = (qown[c, t, z].astype(F32) + qrecv[c, t].astype(F32)).astype(BF)
    drain(len(copies))


def hand_out(out_ref, gq_ref, go_ref, codes, grads, gq, go, out_v, gq_v, go_v, sems):
    rows = gq.shape[0] // 4
    moves = [(gq_ref.at[part], gq_v.at[part], gq.at[part]) for part in (pl.ds(rows * i, rows) for i in range(4))]
    moves.append((go_ref, go_v, go))
    moves += [(out_ref.at[i], out_v.at[i], out) for i, out in enumerate((codes, grads))]
    loads = [pltpu.make_async_copy(a, b, sems.at[0, i]) for i, (a, b, _) in enumerate(moves)]
    stores = [pltpu.make_async_copy(b, c, sems.at[1, i]) for i, (_, b, c) in enumerate(moves)]
    for c in loads:
        c.start()
    for load, store in zip(loads, stores):
        load.wait()
        store.start()
    for c in stores:
        c.wait()


def body(
    transit_latents,
    encoded_arrivals,
    arriving_latent_derivative,
    objective_derivative_arrivals,
    kept_inputs,
    onward_sequence_labels,
    reverse_sequence_labels,
    expander_attn_factors,
    outgoing_compressor_factors,
):
    sections = lax.axis_size("section")
    w, wo = jax.ShapeDtypeStruct(expander_attn_factors.shape[1:], BF), jax.ShapeDtypeStruct(outgoing_compressor_factors.shape[1:], BF)
    feat, cols = w.shape
    heads = cols // (3 * HD)
    toks, shard = transit_latents.shape[1:]
    vm = pl.BlockSpec(memory_space=pltpu.VMEM)
    block = (2, YS, shard, toks)
    hbm = pl.BlockSpec(memory_space=pl.ANY)
    scratch = [
        pltpu.VMEM((2, TICKS - 1, shard, toks), BF),
        pltpu.VMEM(onward_sequence_labels.shape, jnp.int32),
        pltpu.VMEM(reverse_sequence_labels.shape, jnp.int32),
        pltpu.VMEM((feat, cols), BF),
        pltpu.VMEM((heads * HD, feat), BF),
        pltpu.VMEM((3 * TICKS,) + block, BF),
        pltpu.VMEM((2, TICKS) + block, BF),
        pltpu.VMEM((2, TICKS, 2, 2, 4, shard, toks), BF),
        pltpu.VMEM((2, TICKS, 2, 2, shard, toks), BF),
        pltpu.VMEM((2, TICKS, 2, shard, toks), BF),
        pltpu.VMEM((2, TICKS, 2, shard, toks), BF),
        pltpu.VMEM((2, TICKS, shard, toks), BF),
        pltpu.VMEM((cols, feat), BF),
        pltpu.VMEM((feat, heads * HD), BF),
        pltpu.VMEM((TICKS, toks, toks), F32),
        pltpu.VMEM((TICKS, toks, toks), F32),
        pltpu.VMEM((TICKS, feat, toks), BF),
        pltpu.VMEM((TICKS, heads, HD, toks), F32),
        pltpu.VMEM((TICKS, heads, HD, toks), BF),
        pltpu.VMEM((TICKS, heads, HD, toks), BF),
        pltpu.VMEM((TICKS, heads, HD, toks), F32),
        pltpu.VMEM((TICKS, heads, toks, HD), BF),
        pltpu.VMEM((TICKS, heads, toks, toks), F32),
        pltpu.VMEM((TICKS, heads, toks, toks), BF),
        pltpu.VMEM((TICKS, heads * HD, toks), BF),
        pltpu.VMEM((TICKS, heads, 8, toks), F32),
        pltpu.VMEM((TICKS, 1, toks), F32),
        pltpu.VMEM((TICKS, cols, toks), BF),
        pltpu.SemaphoreType.DMA((9,)),
        pltpu.SemaphoreType.DMA((POOL,)),
        pltpu.SemaphoreType.DMA((COPIES,)),
    ]
    out, gq, go = pl.pallas_call(
        functools.partial(kernel, sections),
        out_shape=(
            jax.ShapeDtypeStruct((2, TICKS, shard, toks), BF),
            jax.ShapeDtypeStruct(w.shape, F32),
            jax.ShapeDtypeStruct(wo.shape, F32),
        ),
        in_specs=[hbm] * 9,
        out_specs=(vm, vm, vm),
        scratch_shapes=scratch,
        compiler_params=pltpu.CompilerParams(
            collective_id=0, has_side_effects=True, vmem_limit_bytes=60 * 1024 * 1024
        ),
    )(
        transit_latents.swapaxes(1, 2),
        encoded_arrivals.swapaxes(1, 2),
        arriving_latent_derivative.swapaxes(1, 2),
        objective_derivative_arrivals.swapaxes(1, 2),
        kept_inputs.swapaxes(2, 3),
        onward_sequence_labels,
        reverse_sequence_labels,
        expander_attn_factors,
        outgoing_compressor_factors,
    )
    codes, grads, gq, go = pl.pallas_call(
        hand_out,
        out_shape=(
            jax.ShapeDtypeStruct(out.shape[1:], BF),
            jax.ShapeDtypeStruct(out.shape[1:], BF),
            jax.ShapeDtypeStruct(gq.shape, F32),
            jax.ShapeDtypeStruct(go.shape, F32),
        ),
        in_specs=[hbm] * 3,
        out_specs=[hbm] * 4,
        scratch_shapes=[
            pltpu.VMEM(out.shape, BF),
            pltpu.VMEM(gq.shape, F32),
            pltpu.VMEM(go.shape, F32),
            pltpu.SemaphoreType.DMA((2, 7)),
        ],
        compiler_params=pltpu.CompilerParams(vmem_limit_bytes=60 * 1024 * 1024),
    )(out, gq, go)
    return codes.swapaxes(1, 2)[None], grads.swapaxes(1, 2)[None], gq[None], go[None]


def solution(mesh):
    in_specs = (
        P("section", None, "tensor"),
        P(None, None, "tensor"),
        P("section", None, "tensor"),
        P(None, None, "tensor"),
        P("section", None, None, "tensor"),
        P(),
        P(),
        P("section", None, "tensor"),
        P("section", "tensor", None),
    )
    out_specs = (
        P("section", None, None, "tensor"),
        P("section", None, None, "tensor"),
        P("section", None, "tensor"),
        P("section", "tensor", None),
    )
    return jax.shard_map(body, mesh=mesh, in_specs=in_specs, out_specs=out_specs, check_vma=False)
```
